32 devices in a mesh: img: 8 (over y, x, core), txt: 4 (over z).
Axes of the slice: x: 2, y: 2, z: 4, core: 2. Of those that a mesh axis runs over, the one named last changes fastest.
Arguments:
- images: bfloat16 [768, 512], P('img'), may hold values from -1 to 1
- texts: bfloat16 [768, 512], P(('txt', 'img')), may hold values from -1 to 1
Outputs:
- grad_images: float32 [768, 512], P(('img', 'txt'))
- grad_texts: float32 [768, 512], P(('txt', 'img'))
The draws below stay inside these ranges and needn't reach their ends.
All inputs are finite; a program needn't handle non-finite values.
Results may differ from the reference program's by a relative error of at most 0.0075.
Values may be sent and summed in bfloat16 or wider, within the bound.
A program may use at most 64 MiB of HBM per device.

```python
import math
import jax
import jax.numpy as jnp
from jax import lax

D = 512
ROUNDS = 3
NPAIR = 768


cluster_count = 16


noise_scale = 0.05


def rough_draw(key, shape):
    return jax.random.truncated_normal(key, -4.0, 4.0, shape, jnp.float32)


def shared_parts(key):
    shared_key = jax.random.fold_in(key, 11)
    k_group, k_center, k_noise, k_imgamp, k_txtamp = jax.random.split(shared_key, 5)
    groups = jax.random.randint(k_group, (NPAIR,), 0, cluster_count)
    centers = noise_scale * rough_draw(k_center, (cluster_count, D))
    shared_center = jnp.take(centers, groups, axis=0)
    img_noise = noise_scale * rough_draw(k_noise, (NPAIR, D))
    lowest_amp = 0.3
    img_amp = jax.random.uniform(k_imgamp, (NPAIR, 1), jnp.float32, lowest_amp, 3.0)
    txt_amp = jax.random.uniform(k_txtamp, (NPAIR, 1), jnp.float32, lowest_amp, 3.0)
    return (shared_center, img_noise, img_amp, txt_amp)


def draw_images(key, part):
    shared_center, img_noise, img_amp, txt_amp = shared_parts(key)
    values = img_amp * shared_center + img_noise
    return values.astype(jnp.bfloat16)


def draw_texts(key, part):
    shared_center, img_noise, img_amp, txt_amp = shared_parts(key)
    own_noise = noise_scale * rough_draw(jax.random.fold_in(key, 31), (NPAIR, D))
    values = txt_amp * shared_center + 0.6 * img_noise + 0.8 * own_noise
    return values.astype(jnp.bfloat16)


def setup_inputs(seed: int = 0) -> dict:
    arg_keys = jax.random.split(jax.random.key(seed), 3)
    images = draw_images(jax.random.fold_in(arg_keys[2], 71), 0)
    texts = draw_texts(jax.random.fold_in(arg_keys[2], 71), 0)
    return {"images": images, "texts": texts}


logit_scale = 30.0
mix_weight = 0.5
norm_eps = 1e-06
highest = lax.Precision.HIGHEST

def normalize(values):
    wide = values.astype(jnp.float32)
    length = jnp.sqrt(lax.optimization_barrier(jnp.sum(wide * wide, axis=1, keepdims=True)) + norm_eps)
    return (wide / length, length)

def project_back(grad, unit, length):
    along = lax.optimization_barrier(jnp.sum(unit * grad, axis=1, keepdims=True))
    return (grad - unit * along) / length

def reference(images, texts):
    unit_img, len_img = normalize(images)
    unit_txt, len_txt = normalize(texts)
    img_wide = unit_img.astype(jnp.bfloat16).astype(jnp.float32)
    txt_wide = unit_txt.astype(jnp.bfloat16).astype(jnp.float32)
    total = float(NPAIR)
    block = math.gcd(512, NPAIR)
    count = NPAIR // block
    starts = jnp.arange(count, dtype=jnp.int32) * block

    def kernel_rows(start):
        rows = lax.dynamic_slice_in_dim(img_wide, start, block, 0)
        scores = logit_scale * jnp.dot(rows, txt_wide.T, precision=highest, preferred_element_type=jnp.float32)
        return (rows, jnp.exp(scores - logit_scale))

    def first_pass(carry, start):
        rows, kernel = kernel_rows(start)
        return (carry + lax.optimization_barrier(jnp.sum(kernel, axis=0)), lax.optimization_barrier(jnp.sum(kernel, axis=1)))
    col_total, row_parts = lax.scan(first_pass, jnp.zeros((NPAIR,), jnp.float32), starts)
    row_total = row_parts.reshape(NPAIR)
    col_vec = col_total
    row_weight = jnp.ones((NPAIR,), jnp.float32)
    col_scale = jnp.ones((NPAIR,), jnp.float32)
    for step in range(ROUNDS):
        col_scale = 1.0 / (total * col_vec)

        def round_pass(carry, start, col_scale=col_scale):
            rows, kernel = kernel_rows(start)
            row_sum = jnp.dot(kernel, col_scale, precision=highest)
            weight = 1.0 / (total * row_sum)
            return (carry + jnp.dot(weight, kernel, precision=highest), weight)
        col_vec, weights = lax.scan(round_pass, jnp.zeros((NPAIR,), jnp.float32), starts)
        row_weight = weights.reshape(NPAIR)
    col_weight = 1.0 - mix_weight + mix_weight * total * col_scale * col_vec
    txt_ids = jnp.arange(NPAIR, dtype=jnp.int32)

    def grad_pass(carry, start):
        rows, kernel = kernel_rows(start)
        img_ids = start + jnp.arange(block, dtype=jnp.int32)
        eye = (img_ids[:, None] == txt_ids[None, :]).astype(jnp.float32)
        weight = lax.dynamic_slice_in_dim(row_weight, start, block, 0)
        rtot = lax.dynamic_slice_in_dim(row_total, start, block, 0)
        target = (1.0 - mix_weight) * eye + mix_weight * total * weight[:, None] * kernel * col_scale[None, :]
        grad_logit = 0.5 * (kernel / rtot[:, None] + col_weight[None, :] * kernel / col_total[None, :] - 2.0 * target)
        grad_wide = grad_logit.astype(jnp.bfloat16).astype(jnp.float32)
        g_rows = logit_scale * jnp.dot(grad_wide, txt_wide, precision=highest)
        g_cols = logit_scale * jnp.dot(grad_wide.T, rows, precision=highest)
        return (carry + g_cols, g_rows)
    g_txt, g_parts = lax.scan(grad_pass, jnp.zeros((NPAIR, D), jnp.float32), starts)
    g_img = g_parts.reshape(NPAIR, D)
    return (project_back(g_img, unit_img, len_img), project_back(g_txt, unit_txt, len_txt))
```

```python
import jax
import jax.numpy as jnp
from jax import lax
from jax.experimental import pallas as pl
from jax.experimental.pallas import tpu as pltpu
from jax.sharding import PartitionSpec as P

ROUNDS = 3


logit_scale = 30.0
mix_weight = 0.5
norm_eps = 1e-06
highest = lax.Precision.HIGHEST


def normalize(values):
    wide = values.astype(jnp.float32)
    length = jnp.sqrt(jnp.sum(wide * wide, axis=1, keepdims=True) + norm_eps)
    return (wide / length, length)


def project_back(grad, unit, length):
    along = jnp.sum(unit * grad, axis=1, keepdims=True)
    return (grad - unit * along) / length


def shards(images, texts):
    own_rows = texts.shape[0]
    img_block = images.shape[0]
    img_index = lax.axis_index("img")
    txt_index = lax.axis_index("txt")
    unit_img, len_img = normalize(images)
    img_bf = unit_img.astype(jnp.bfloat16)
    unit_txt, len_txt = normalize(texts)
    txt_bf = lax.all_gather(unit_txt.astype(jnp.bfloat16), "img", axis=0, tiled=True)
    txt_block = txt_bf.shape[0]
    total = float(img_block * lax.axis_size("img"))
    scores = logit_scale * lax.dot_general(
        img_bf, txt_bf, (((1,), (1,)), ((), ())), preferred_element_type=jnp.float32
    )
    kernel = jnp.exp(scores - logit_scale)
    row_weight = jnp.ones((img_block,), jnp.float32)
    col_scale = jnp.ones((txt_block,), jnp.float32)
    col_total = col_scale
    row_total = row_weight
    last_cols = col_scale
    for step in range(ROUNDS + 1):
        col_part = jnp.dot(row_weight, kernel, precision=highest)
        col_sum = lax.psum(col_part, "img")
        if step == 0:
            col_total = col_sum
        if step == ROUNDS:
            last_cols = col_sum
        else:
            col_scale = 1.0 / (total * col_sum)
            row_part = jnp.dot(kernel, col_scale, precision=highest)
            if step == 0:
                stats = jnp.stack([row_part, jnp.sum(kernel, axis=1)])
            else:
                stats = row_part[None, :]
            summed = lax.psum(stats, "txt")
            if step == 0:
                row_total = summed[1]
            row_weight = 1.0 / (total * summed[0])
    col_weight = 1.0 - mix_weight + mix_weight * total * col_scale * last_cols
    img_ids = img_index * img_block + jnp.arange(img_block, dtype=jnp.int32)
    txt_ids = txt_index * txt_block + jnp.arange(txt_block, dtype=jnp.int32)
    eye = (img_ids[:, None] == txt_ids[None, :]).astype(jnp.float32)
    target = (1.0 - mix_weight) * eye + mix_weight * total * row_weight[
        :, None
    ] * kernel * col_scale[None, :]
    grad_logit = 0.5 * (
        kernel / row_total[:, None]
        + col_weight[None, :] * kernel / col_total[None, :]
        - 2.0 * target
    )
    grad_logit = grad_logit.astype(jnp.bfloat16)
    g_img = lax.psum_scatter(
        logit_scale * jnp.dot(grad_logit, txt_bf, preferred_element_type=jnp.float32),
        "txt",
        scatter_dimension=0,
        tiled=True,
    )
    g_txt = lax.psum_scatter(
        logit_scale
        * lax.dot_general(
            grad_logit, img_bf, (((0,), (0,)), ((), ())), preferred_element_type=jnp.float32
        ),
        "img",
        scatter_dimension=0,
        tiled=True,
    )
    own_unit = lax.dynamic_slice_in_dim(unit_img, txt_index * own_rows, own_rows, 0)
    own_len = lax.dynamic_slice_in_dim(len_img, txt_index * own_rows, own_rows, 0)
    grad_images = project_back(g_img, own_unit, own_len)
    grad_texts = project_back(g_txt, unit_txt, len_txt)
    return (grad_images, grad_texts)


MESH = pl.DeviceIdType.MESH
F32 = jnp.float32
BF16 = jnp.bfloat16


def nt_dot(left, right):
    return lax.dot_general(
        left, right, (((1,), (1,)), ((), ())), preferred_element_type=F32
    )


def scaled_kernel(left, right):
    return jnp.exp(logit_scale * nt_dot(left, right) - logit_scale)


def fold_rows(values):
    rows, cols = values.shape
    return jnp.sum(values.reshape(rows // 8, 8, cols), axis=0)


def gathered_body(
    images_ref,
    texts_ref,
    gimg_ref,
    gtxt_ref,
    img_buf,
    txt_buf,
    col_in,
    wide_img,
    kt,
    k_own,
    col_total_ref,
    scale_ref,
    send_sem,
    img_recv,
    txt_recv,
    col_recv,
):
    slots, slot_rows, width = img_buf.shape
    depth, own = col_in.shape[0], texts_ref.shape[0]
    half = width // 2
    total_rows = slots * slot_rows
    total = float(total_rows)

    me = lax.axis_index("img")
    layer = lax.axis_index("txt")
    core = me % 2
    x = (me // 2) % 2
    y = me // 4
    first = (y + core * (1 - 2 * y)) * 4 + (x + (1 - core) * (1 - 2 * x)) * 2 + core
    second = (y + (1 - core) * (1 - 2 * y)) * 4 + (x + core * (1 - 2 * x)) * 2 + core
    across = (1 - y) * 4 + (1 - x) * 2 + core
    sibling = me + 1 - 2 * core
    flip = 1 - 2 * core

    barrier = pltpu.get_barrier_semaphore()
    for peer in (first, second, sibling):
        pl.semaphore_signal(barrier, inc=1, device_id=(peer, layer), device_id_type=MESH)
    for step in range(1, depth):
        pl.semaphore_signal(
            barrier, inc=1, device_id=(me, (layer + step) % depth), device_id_type=MESH
        )

    unit_txt, len_txt = normalize(texts_ref[...])
    col_in[layer] = jnp.concatenate([unit_txt[:, :half], unit_txt[:, half:]], axis=0).astype(
        BF16
    )
    wide = images_ref[...].astype(F32)
    wide_img[...] = wide
    unit_all, _ = normalize(wide)
    img_buf[me] = unit_all.astype(BF16)

    pl.semaphore_wait(barrier, 2 + depth)

    started = []

    def send(buf, slot, recv, device):
        copy = pltpu.make_async_remote_copy(
            src_ref=buf.at[slot],
            dst_ref=buf.at[slot],
            send_sem=send_sem.at[len(started)],
            recv_sem=recv.at[slot],
            device_id=device,
            device_id_type=MESH,
        )
        copy.start()
        started.append(copy)

    def arrive(buf, slot, recv):
        pltpu.make_async_remote_copy(
            src_ref=buf.at[slot],
            dst_ref=buf.at[slot],
            send_sem=send_sem.at[0],
            recv_sem=recv.at[slot],
            device_id=(sibling, layer),
            device_id_type=MESH,
        ).wait_recv()

    for step in range(1, depth):
        send(col_in, layer, col_recv, (me, (layer + step) % depth))
    for peer in (first, second, sibling):
        send(img_buf, me, img_recv, (peer, layer))

    arrive(img_buf, first, img_recv)
    send(img_buf, first, img_recv, (second, layer))
    send(img_buf, first, img_recv, (sibling, layer))

    for step in range(1, depth):
        arrive(col_in, (layer + step) % depth, col_recv)
    pieces = []
    for z in range(depth):
        block = col_in[z].astype(F32)
        pieces.append(jnp.concatenate([block[:own], block[own:]], axis=1))
    txt_buf[me] = jnp.concatenate(pieces, axis=0).astype(BF16)
    for peer in (first, second, sibling):
        send(txt_buf, me, txt_recv, (peer, layer))

    arrive(img_buf, second, img_recv)
    send(img_buf, second, img_recv, (sibling, layer))
    arrive(img_buf, across, img_recv)
    send(img_buf, across, img_recv, (sibling, layer))
    arrive(img_buf, sibling, img_recv)
    for slot in (first, second, across):
        arrive(img_buf, slot + flip, img_recv)

    img_all = img_buf[...].reshape(total_rows, width)
    own_raw = wide_img[pl.ds(pl.multiple_of(layer * own, 8), own), :]
    own_img, len_img = normalize(own_raw)
    own_img_bf = own_img.astype(BF16)

    row_acc = jnp.zeros((8, total_rows), F32)
    row_sum = jnp.zeros((8, total_rows), F32)

    def absorb(slot, row_acc, row_sum):
        block = txt_buf[slot]
        values = scaled_kernel(block, img_all)
        kt[slot] = values
        k_own[slot] = scaled_kernel(block, own_img_bf)
        cols = jnp.sum(values, axis=1, keepdims=True)
        col_total_ref[slot] = cols
        return row_acc + fold_rows(values * (1.0 / (total * cols))), row_sum + fold_rows(values)

    row_acc, row_sum = absorb(me, row_acc, row_sum)
    arrive(txt_buf, sibling, txt_recv)
    row_acc, row_sum = absorb(sibling, row_acc, row_sum)
    arrive(txt_buf, first, txt_recv)
    send(txt_buf, first, txt_recv, (second, layer))
    send(txt_buf, first, txt_recv, (sibling, layer))
    row_acc, row_sum = absorb(first, row_acc, row_sum)
    arrive(txt_buf, second, txt_recv)
    send(txt_buf, second, txt_recv, (sibling, layer))
    row_acc, row_sum = absorb(second, row_acc, row_sum)
    arrive(txt_buf, second + flip, txt_recv)
    row_acc, row_sum = absorb(second + flip, row_acc, row_sum)
    arrive(txt_buf, first + flip, txt_recv)
    row_acc, row_sum = absorb(first + flip, row_acc, row_sum)
    arrive(txt_buf, across, txt_recv)
    send(txt_buf, across, txt_recv, (sibling, layer))
    row_acc, row_sum = absorb(across, row_acc, row_sum)
    arrive(txt_buf, across + flip, txt_recv)
    row_acc, row_sum = absorb(across + flip, row_acc, row_sum)

    row_total = jnp.sum(row_sum, axis=0, keepdims=True)
    row_weight = 1.0 / (total * jnp.sum(row_acc, axis=0, keepdims=True))
    previous = row_weight
    for step in range(1, ROUNDS):
        previous = row_weight
        row_acc = jnp.zeros((8, total_rows), F32)
        for slot in range(slots):
            scale = 1.0 / (total * jnp.sum(kt[slot] * row_weight, axis=1, keepdims=True))
            row_acc += fold_rows(kt[slot] * scale)
            scale_ref[slot] = scale
        row_weight = 1.0 / (total * jnp.sum(row_acc, axis=0, keepdims=True))

    keep = 1.0 - mix_weight
    col_scale = scale_ref[...].reshape(total_rows, 1)
    col_total = col_total_ref[...].reshape(total_rows, 1)
    last_cols = jnp.concatenate(
        [jnp.sum(kt[slot] * row_weight, axis=1, keepdims=True) for slot in range(slots)], axis=0
    )
    col_weight = keep + mix_weight * total * col_scale * last_cols
    values = k_own[...].reshape(total_rows, own)
    own_total = jnp.sum(values, axis=0, keepdims=True)
    own_weight = 1.0 / (total * jnp.sum(values * col_scale, axis=0, keepdims=True))
    group = me * depth + layer
    place = (group % slots) * slot_rows + (group // slots) * own
    at_row = lax.broadcasted_iota(jnp.int32, (total_rows, own), 0)
    at_col = lax.broadcasted_iota(jnp.int32, (total_rows, own), 1)
    eye = (at_row == at_col + place).astype(F32)
    factor = 1.0 / own_total + col_weight / col_total - (2.0 * mix_weight * total) * (
        own_weight * col_scale
    )
    grad_logit = (0.5 * (values * factor - (2.0 * keep) * eye)).astype(BF16)
    txt_all = txt_buf[...].reshape(total_rows, width)
    g_img = logit_scale * lax.dot_general(
        grad_logit, txt_all, (((0,), (0,)), ((), ())), preferred_element_type=F32
    )
    gimg_ref[...] = project_back(g_img, own_img, len_img)

    values = scaled_kernel(unit_txt.astype(BF16), img_all)
    own_total = jnp.sum(values, axis=1, keepdims=True)
    own_scale = 1.0 / (total * jnp.sum(values * previous, axis=1, keepdims=True))
    own_cols = jnp.sum(values * row_weight, axis=1, keepdims=True)
    own_col_weight = keep + mix_weight * total * own_scale * own_cols
    place = layer * (slots * own) + me * own
    at_row = lax.broadcasted_iota(jnp.int32, (own, total_rows), 0)
    at_col = lax.broadcasted_iota(jnp.int32, (own, total_rows), 1)
    eye = (at_col == at_row + place).astype(F32)
    factor = 1.0 / row_total + own_col_weight / own_total - (2.0 * mix_weight * total) * (
        row_weight * own_scale
    )
    grad_logit = (0.5 * (values * factor - (2.0 * keep) * eye)).astype(BF16)
    g_txt = logit_scale * jnp.dot(grad_logit, img_all, preferred_element_type=F32)
    gtxt_ref[...] = project_back(g_txt, unit_txt, len_txt)

    for copy in started:
        copy.wait_send()


def gathered(slots, depth, images, texts):
    slot_rows, width = images.shape
    own = texts.shape[0]
    total_rows = slots * slot_rows
    vmem = pl.BlockSpec(memory_space=pltpu.VMEM)
    out = jax.ShapeDtypeStruct((own, width), F32)
    return pl.pallas_call(
        gathered_body,
        out_shape=(out, out),
        in_specs=[vmem, vmem],
        out_specs=(vmem, vmem),
        scratch_shapes=[
            pltpu.VMEM((slots, slot_rows, width), BF16),
            pltpu.VMEM((slots, slot_rows, width), BF16),
            pltpu.VMEM((depth, 2 * own, width // 2), BF16),
            pltpu.VMEM((slot_rows, width), F32),
            pltpu.VMEM((slots, slot_rows, total_rows), F32),
            pltpu.VMEM((slots, slot_rows, own), F32),
            pltpu.VMEM((slots, slot_rows, 1), F32),
            pltpu.VMEM((slots, slot_rows, 1), F32),
            pltpu.SemaphoreType.DMA((depth - 1 + 14,)),
            pltpu.SemaphoreType.DMA((slots,)),
            pltpu.SemaphoreType.DMA((slots,)),
            pltpu.SemaphoreType.DMA((depth,)),
        ],
        compiler_params=pltpu.CompilerParams(
            collective_id=0, has_side_effects=True, vmem_limit_bytes=32 * 1024 * 1024
        ),
    )(images, texts)


def solution(mesh):
    placed = (P("img", None), P(("txt", "img"), None))
    slots, depth = mesh.shape["img"], mesh.shape["txt"]

    def body(images, texts):
        pairs = images.shape[0] * slots
        whole = slots == 8 and images.shape[0] % 16 == 0 and texts.shape[0] % 8 == 0
        if whole and pairs * pairs * 4 <= 4 * 1024 * 1024:
            return gathered(slots, depth, images, texts)
        return shards(images, texts)

    return jax.shard_map(
        body,
        mesh=mesh,
        in_specs=placed,
        out_specs=(P(("img", "txt"), None), P(("txt", "img"), None)),
        check_vma=False,
    )
```

```python
import jax
import jax.numpy as jnp
from jax import lax
from jax.experimental import pallas as pl
from jax.experimental.pallas import tpu as pltpu
from jax.sharding import PartitionSpec as P

ROUNDS = 3


logit_scale = 30.0
mix_weight = 0.5
norm_eps = 1e-06
highest = lax.Precision.HIGHEST


def normalize(values):
    wide = values.astype(jnp.float32)
    length = jnp.sqrt(jnp.sum(wide * wide, axis=1, keepdims=True) + norm_eps)
    return (wide / length, length)


def project_back(grad, unit, length):
    along = jnp.sum(unit * grad, axis=1, keepdims=True)
    return (grad - unit * along) / length


def shards(images, texts):
    own_rows = texts.shape[0]
    img_block = images.shape[0]
    img_index = lax.axis_index("img")
    txt_index = lax.axis_index("txt")
    unit_img, len_img = normalize(images)
    img_bf = unit_img.astype(jnp.bfloat16)
    unit_txt, len_txt = normalize(texts)
    txt_bf = lax.all_gather(unit_txt.astype(jnp.bfloat16), "img", axis=0, tiled=True)
    txt_block = txt_bf.shape[0]
    total = float(img_block * lax.axis_size("img"))
    scores = logit_scale * lax.dot_general(
        img_bf, txt_bf, (((1,), (1,)), ((), ())), preferred_element_type=jnp.float32
    )
    kernel = jnp.exp(scores - logit_scale)
    row_weight = jnp.ones((img_block,), jnp.float32)
    col_scale = jnp.ones((txt_block,), jnp.float32)
    col_total = col_scale
    row_total = row_weight
    last_cols = col_scale
    for step in range(ROUNDS + 1):
        col_part = jnp.dot(row_weight, kernel, precision=highest)
        col_sum = lax.psum(col_part, "img")
        if step == 0:
            col_total = col_sum
        if step == ROUNDS:
            last_cols = col_sum
        else:
            col_scale = 1.0 / (total * col_sum)
            row_part = jnp.dot(kernel, col_scale, precision=highest)
            if step == 0:
                stats = jnp.stack([row_part, jnp.sum(kernel, axis=1)])
            else:
                stats = row_part[None, :]
            summed = lax.psum(stats, "txt")
            if step == 0:
                row_total = summed[1]
            row_weight = 1.0 / (total * summed[0])
    col_weight = 1.0 - mix_weight + mix_weight * total * col_scale * last_cols
    img_ids = img_index * img_block + jnp.arange(img_block, dtype=jnp.int32)
    txt_ids = txt_index * txt_block + jnp.arange(txt_block, dtype=jnp.int32)
    eye = (img_ids[:, None] == txt_ids[None, :]).astype(jnp.float32)
    target = (1.0 - mix_weight) * eye + mix_weight * total * row_weight[
        :, None
    ] * kernel * col_scale[None, :]
    grad_logit = 0.5 * (
        kernel / row_total[:, None]
        + col_weight[None, :] * kernel / col_total[None, :]
        - 2.0 * target
    )
    grad_logit = grad_logit.astype(jnp.bfloat16)
    g_img = lax.psum_scatter(
        logit_scale * jnp.dot(grad_logit, txt_bf, preferred_element_type=jnp.float32),
        "txt",
        scatter_dimension=0,
        tiled=True,
    )
    g_txt = lax.psum_scatter(
        logit_scale
        * lax.dot_general(
            grad_logit, img_bf, (((0,), (0,)), ((), ())), preferred_element_type=jnp.float32
        ),
        "img",
        scatter_dimension=0,
        tiled=True,
    )
    own_unit = lax.dynamic_slice_in_dim(unit_img, txt_index * own_rows, own_rows, 0)
    own_len = lax.dynamic_slice_in_dim(len_img, txt_index * own_rows, own_rows, 0)
    grad_images = project_back(g_img, own_unit, own_len)
    grad_texts = project_back(g_txt, unit_txt, len_txt)
    return (grad_images, grad_texts)


MESH = pl.DeviceIdType.MESH
F32 = jnp.float32
BF16 = jnp.bfloat16


def nt_dot(left, right):
    return lax.dot_general(
        left, right, (((1,), (1,)), ((), ())), preferred_element_type=F32
    )


def scaled_kernel(left, right):
    return jnp.exp(logit_scale * nt_dot(left, right) - logit_scale)


def fold_rows(values):
    rows, cols = values.shape
    return jnp.sum(values.reshape(rows // 8, 8, cols), axis=0)


def gathered_body(
    images_ref,
    texts_ref,
    gimg_ref,
    gtxt_ref,
    img_buf,
    txt_buf,
    col_in,
    wide_img,
    raw_img,
    raw_txt,
    kt,
    first_scale,
    send_sem,
    img_recv,
    txt_recv,
    col_recv,
    load_sem,
):
    slots, slot_rows, width = img_buf.shape
    depth, own = col_in.shape[0], texts_ref.shape[0]
    half = width // 2
    total_rows = slots * slot_rows
    chunks = img_recv.shape[1]
    piece = slot_rows // chunks

    load_txt = pltpu.make_async_copy(texts_ref, raw_txt, load_sem.at[0])
    load_txt.start()
    load_img = pltpu.make_async_copy(images_ref, raw_img, load_sem.at[1])
    load_img.start()

    me = lax.axis_index("img")
    layer = lax.axis_index("txt")
    core = me % 2
    x = (me // 2) % 2
    y = me // 4
    first = (y + core * (1 - 2 * y)) * 4 + (x + (1 - core) * (1 - 2 * x)) * 2 + core
    second = (y + (1 - core) * (1 - 2 * y)) * 4 + (x + core * (1 - 2 * x)) * 2 + core
    across = (1 - y) * 4 + (1 - x) * 2 + core
    flip = 1 - 2 * core
    sibling = me + flip

    barrier = pltpu.get_barrier_semaphore()
    for peer in (first, second, sibling):
        pl.semaphore_signal(barrier, inc=1, device_id=(peer, layer), device_id_type=MESH)
    for step in range(1, depth):
        pl.semaphore_signal(
            barrier, inc=1, device_id=(me, (layer + step) % depth), device_id_type=MESH
        )

    load_txt.wait()
    unit_txt, len_txt = normalize(raw_txt[...])
    col_in[layer] = jnp.concatenate([unit_txt[:, :half], unit_txt[:, half:]], axis=0).astype(
        BF16
    )
    load_img.wait()
    wide = raw_img[...].astype(F32)
    wide_img[...] = wide
    unit_all, _ = normalize(wide)
    img_buf[me] = unit_all.astype(BF16)

    pl.semaphore_wait(barrier, 2 + depth)

    started = []

    def push(src, dst, recv, device):
        copy = pltpu.make_async_remote_copy(
            src_ref=src,
            dst_ref=dst,
            send_sem=send_sem.at[len(started)],
            recv_sem=recv,
            device_id=device,
            device_id_type=MESH,
        )
        copy.start()
        started.append(copy)

    def part(buf, slot, chunk):
        return buf.at[slot, pl.ds(chunk * piece, piece)]

    def send(buf, slot, chunk, recv, *peers):
        for peer in peers:
            ref = part(buf, slot, chunk)
            push(ref, ref, recv.at[slot, chunk], (peer, layer))

    def landed(ref, recv):
        pltpu.make_async_remote_copy(
            src_ref=ref,
            dst_ref=ref,
            send_sem=send_sem.at[0],
            recv_sem=recv,
            device_id=(sibling, layer),
            device_id_type=MESH,
        ).wait_recv()

    def arrive(buf, slot, recv, *peers):
        for chunk in range(chunks):
            landed(part(buf, slot, chunk), recv.at[slot, chunk])
            send(buf, slot, chunk, recv, *peers)

    for step in range(1, depth):
        push(
            col_in.at[layer],
            col_in.at[layer],
            col_recv.at[layer],
            (me, (layer + step) % depth),
        )
    for chunk in range(chunks):
        send(img_buf, me, chunk, img_recv, first, second)
    for chunk in range(chunks):
        send(img_buf, me, chunk, img_recv, sibling)

    arrive(img_buf, first, img_recv, second, sibling)
    for step in range(1, depth):
        source = (layer + step) % depth
        landed(col_in.at[source], col_recv.at[source])
    pieces = []
    for z in range(depth):
        block = col_in[z].astype(F32)
        pieces.append(jnp.concatenate([block[:own], block[own:]], axis=1))
    txt_buf[me] = jnp.concatenate(pieces, axis=0).astype(BF16)
    for chunk in range(chunks):
        send(txt_buf, me, chunk, txt_recv, first, second)
    for chunk in range(chunks):
        send(txt_buf, me, chunk, txt_recv, sibling)

    arrive(img_buf, second, img_recv, sibling)
    arrive(img_buf, across, img_recv, sibling)
    arrive(txt_buf, first, txt_recv, second, sibling)
    for slot in (sibling, second + flip, first + flip, across + flip):
        arrive(img_buf, slot, img_recv)

    img_all = img_buf[...].reshape(total_rows, width)
    own_raw = wide_img[pl.ds(pl.multiple_of(layer * own, 8), own), :]
    own_img, len_img = normalize(own_raw)

    row_acc = jnp.zeros((8, total_rows), F32)
    row_sum = jnp.zeros((8, total_rows), F32)

    def absorb(start, count, row_acc, row_sum):
        block = txt_buf[pl.ds(start, count)].reshape(count * slot_rows, width)
        values = scaled_kernel(block, img_all)
        kt[pl.ds(start, count)] = values.reshape(count, slot_rows, total_rows)
        scale = 1.0 / jnp.sum(values, axis=1, keepdims=True)
        first_scale[pl.ds(start, count)] = scale.reshape(count, slot_rows, 1)
        return row_acc + fold_rows(values * scale), row_sum + fold_rows(values)

    arrive(txt_buf, sibling, txt_recv)
    row_acc, row_sum = absorb(me - core, 2, row_acc, row_sum)
    arrive(txt_buf, second, txt_recv, sibling)
    arrive(txt_buf, first + flip, txt_recv)
    row_acc, row_sum = absorb(first - core, 2, row_acc, row_sum)
    arrive(txt_buf, across, txt_recv, sibling)
    arrive(txt_buf, second + flip, txt_recv)
    row_acc, row_sum = absorb(second - core, 2, row_acc, row_sum)
    row_acc, row_sum = absorb(across, 1, row_acc, row_sum)
    arrive(txt_buf, across + flip, txt_recv)
    row_acc, row_sum = absorb(across + flip, 1, row_acc, row_sum)

    row_total = jnp.sum(row_sum, axis=0, keepdims=True)
    row_weight = 1.0 / jnp.sum(row_acc, axis=0, keepdims=True)
    previous = row_weight
    scales = []
    for step in range(1, ROUNDS):
        previous = row_weight
        row_acc = jnp.zeros((8, total_rows), F32)
        scales = []
        for slot in range(slots):
            scale = 1.0 / jnp.sum(kt[slot] * row_weight, axis=1, keepdims=True)
            row_acc += fold_rows(kt[slot] * scale)
            scales.append(scale)
        row_weight = 1.0 / jnp.sum(row_acc, axis=0, keepdims=True)

    keep = 1.0 - mix_weight
    lane = lax.broadcasted_iota(jnp.int32, (slot_rows, 128), 1)
    packed = []
    for slot in range(slots):
        last_cols = jnp.sum(kt[slot] * row_weight, axis=1, keepdims=True)
        weight = (keep + mix_weight * scales[slot] * last_cols) * first_scale[slot]
        packed.append(jnp.where(lane < 64, scales[slot], weight))
    packed = jnp.concatenate(packed, axis=0).T
    col_scale = packed[0:1]
    col_part = packed[64:65]

    at_row = lax.broadcasted_iota(jnp.int32, (own, total_rows), 0)
    at_col = lax.broadcasted_iota(jnp.int32, (own, total_rows), 1)

    def logit_grad(values, factor, place):
        eye = (at_col == at_row + place).astype(F32)
        return (0.5 * (values * factor - (2.0 * keep) * eye)).astype(BF16)

    values = scaled_kernel(unit_txt.astype(BF16), img_all)
    own_total = jnp.sum(values, axis=1, keepdims=True)
    own_scale = 1.0 / jnp.sum(values * previous, axis=1, keepdims=True)
    own_cols = jnp.sum(values * row_weight, axis=1, keepdims=True)
    own_part = (keep + mix_weight * own_scale * own_cols) / own_total
    factor = 1.0 / row_total + own_part - (2.0 * mix_weight) * (row_weight * own_scale)
    grad_logit = logit_grad(values, factor, layer * (slots * own) + me * own)
    g_txt = logit_scale * jnp.dot(grad_logit, img_all, preferred_element_type=F32)
    gtxt_ref[...] = project_back(g_txt, unit_txt, len_txt)

    txt_all = txt_buf[...].reshape(total_rows, width)
    values = scaled_kernel(own_img.astype(BF16), txt_all)
    own_total = jnp.sum(values, axis=1, keepdims=True)
    own_weight = 1.0 / jnp.sum(values * col_scale, axis=1, keepdims=True)
    group = me * depth + layer
    place = (group % slots) * slot_rows + (group // slots) * own
    factor = 1.0 / own_total + col_part - (2.0 * mix_weight) * (own_weight * col_scale)
    grad_logit = logit_grad(values, factor, place)
    g_img = logit_scale * jnp.dot(grad_logit, txt_all, preferred_element_type=F32)
    gimg_ref[...] = project_back(g_img, own_img, len_img)

    for copy in started:
        copy.wait_send()


def gathered(slots, depth, images, texts):
    slot_rows, width = images.shape
    own = texts.shape[0]
    total_rows = slots * slot_rows
    chunks = 2
    vmem = pl.BlockSpec(memory_space=pltpu.VMEM)
    anywhere = pl.BlockSpec(memory_space=pltpu.HBM)
    out = jax.ShapeDtypeStruct((own, width), F32)
    return pl.pallas_call(
        gathered_body,
        out_shape=(out, out),
        in_specs=[anywhere, anywhere],
        out_specs=(vmem, vmem),
        scratch_shapes=[
            pltpu.VMEM((slots, slot_rows, width), BF16),
            pltpu.VMEM((slots, slot_rows, width), BF16),
            pltpu.VMEM((depth, 2 * own, width // 2), BF16),
            pltpu.VMEM((slot_rows, width), F32),
            pltpu.VMEM((slot_rows, width), BF16),
            pltpu.VMEM((own, width), BF16),
            pltpu.VMEM((slots, slot_rows, total_rows), F32),
            pltpu.VMEM((slots, slot_rows, 1), F32),
            pltpu.SemaphoreType.DMA((depth - 1 + 14 * chunks,)),
            pltpu.SemaphoreType.DMA((slots, chunks)),
            pltpu.SemaphoreType.DMA((slots, chunks)),
            pltpu.SemaphoreType.DMA((depth,)),
            pltpu.SemaphoreType.DMA((2,)),
        ],
        compiler_params=pltpu.CompilerParams(
            collective_id=0, has_side_effects=True, vmem_limit_bytes=32 * 1024 * 1024
        ),
    )(images, texts)


def solution(mesh):
    placed = (P("img", None), P(("txt", "img"), None))
    slots, depth = mesh.shape["img"], mesh.shape["txt"]

    def body(images, texts):
        pairs = images.shape[0] * slots
        whole = slots == 8 and images.shape[0] % 32 == 0 and texts.shape[0] % 8 == 0
        if whole and pairs * pairs * 4 <= 4 * 1024 * 1024:
            return gathered(slots, depth, images, texts)
        return shards(images, texts)

    return jax.shard_map(
        body,
        mesh=mesh,
        in_specs=placed,
        out_specs=(P(("img", "txt"), None), P(("txt", "img"), None)),
        check_vma=False,
    )
```

```python
import jax
import jax.numpy as jnp
from jax import lax
from jax.experimental import pallas as pl
from jax.experimental.pallas import tpu as pltpu
from jax.sharding import PartitionSpec as P

ROUNDS = 3


logit_scale = 30.0
mix_weight = 0.5
norm_eps = 1e-06
highest = lax.Precision.HIGHEST


def normalize(values):
    wide = values.astype(jnp.float32)
    length = jnp.sqrt(jnp.sum(wide * wide, axis=1, keepdims=True) + norm_eps)
    return (wide / length, length)


def project_back(grad, unit, length):
    along = jnp.sum(unit * grad, axis=1, keepdims=True)
    return (grad - unit * along) / length


def shards(images, texts):
    own_rows = texts.shape[0]
    img_block = images.shape[0]
    img_index = lax.axis_index("img")
    txt_index = lax.axis_index("txt")
    unit_img, len_img = normalize(images)
    img_bf = unit_img.astype(jnp.bfloat16)
    unit_txt, len_txt = normalize(texts)
    txt_bf = lax.all_gather(unit_txt.astype(jnp.bfloat16), "img", axis=0, tiled=True)
    txt_block = txt_bf.shape[0]
    total = float(img_block * lax.axis_size("img"))
    scores = logit_scale * lax.dot_general(
        img_bf, txt_bf, (((1,), (1,)), ((), ())), preferred_element_type=jnp.float32
    )
    kernel = jnp.exp(scores - logit_scale)
    row_weight = jnp.ones((img_block,), jnp.float32)
    col_scale = jnp.ones((txt_block,), jnp.float32)
    col_total = col_scale
    row_total = row_weight
    last_cols = col_scale
    for step in range(ROUNDS + 1):
        col_part = jnp.dot(row_weight, kernel, precision=highest)
        col_sum = lax.psum(col_part, "img")
        if step == 0:
            col_total = col_sum
        if step == ROUNDS:
            last_cols = col_sum
        else:
            col_scale = 1.0 / (total * col_sum)
            row_part = jnp.dot(kernel, col_scale, precision=highest)
            if step == 0:
                stats = jnp.stack([row_part, jnp.sum(kernel, axis=1)])
            else:
                stats = row_part[None, :]
            summed = lax.psum(stats, "txt")
            if step == 0:
                row_total = summed[1]
            row_weight = 1.0 / (total * summed[0])
    col_weight = 1.0 - mix_weight + mix_weight * total * col_scale * last_cols
    img_ids = img_index * img_block + jnp.arange(img_block, dtype=jnp.int32)
    txt_ids = txt_index * txt_block + jnp.arange(txt_block, dtype=jnp.int32)
    eye = (img_ids[:, None] == txt_ids[None, :]).astype(jnp.float32)
    target = (1.0 - mix_weight) * eye + mix_weight * total * row_weight[
        :, None
    ] * kernel * col_scale[None, :]
    grad_logit = 0.5 * (
        kernel / row_total[:, None]
        + col_weight[None, :] * kernel / col_total[None, :]
        - 2.0 * target
    )
    grad_logit = grad_logit.astype(jnp.bfloat16)
    g_img = lax.psum_scatter(
        logit_scale * jnp.dot(grad_logit, txt_bf, preferred_element_type=jnp.float32),
        "txt",
        scatter_dimension=0,
        tiled=True,
    )
    g_txt = lax.psum_scatter(
        logit_scale
        * lax.dot_general(
            grad_logit, img_bf, (((0,), (0,)), ((), ())), preferred_element_type=jnp.float32
        ),
        "img",
        scatter_dimension=0,
        tiled=True,
    )
    own_unit = lax.dynamic_slice_in_dim(unit_img, txt_index * own_rows, own_rows, 0)
    own_len = lax.dynamic_slice_in_dim(len_img, txt_index * own_rows, own_rows, 0)
    grad_images = project_back(g_img, own_unit, own_len)
    grad_texts = project_back(g_txt, unit_txt, len_txt)
    return (grad_images, grad_texts)


MESH = pl.DeviceIdType.MESH
F32 = jnp.float32
BF16 = jnp.bfloat16


def nt_dot(left, right):
    return lax.dot_general(
        left, right, (((1,), (1,)), ((), ())), preferred_element_type=F32
    )


def scaled_kernel(left, right):
    return jnp.exp(logit_scale * nt_dot(left, right) - logit_scale)


def fold_rows(values):
    rows, cols = values.shape
    return jnp.sum(values.reshape(rows // 8, 8, cols), axis=0)


def gathered_body(
    images_ref,
    texts_ref,
    gimg_ref,
    gtxt_ref,
    img_buf,
    txt_buf,
    col_in,
    wide_img,
    raw_img,
    raw_txt,
    kt,
    first_scale,
    send_sem,
    img_recv,
    txt_recv,
    col_recv,
    load_sem,
):
    slots, slot_rows, width = img_buf.shape
    depth, own = col_in.shape[0], texts_ref.shape[0]
    half = width // 2
    total_rows = slots * slot_rows
    chunks = img_recv.shape[1]
    piece = slot_rows // chunks

    load_txt = pltpu.make_async_copy(texts_ref, raw_txt, load_sem.at[0])
    load_txt.start()
    load_img = pltpu.make_async_copy(images_ref, raw_img, load_sem.at[1])
    load_img.start()

    me = lax.axis_index("img")
    layer = lax.axis_index("txt")
    core = me % 2
    x = (me // 2) % 2
    y = me // 4
    first = (y + core * (1 - 2 * y)) * 4 + (x + (1 - core) * (1 - 2 * x)) * 2 + core
    second = (y + (1 - core) * (1 - 2 * y)) * 4 + (x + core * (1 - 2 * x)) * 2 + core
    across = (1 - y) * 4 + (1 - x) * 2 + core
    flip = 1 - 2 * core
    sibling = me + flip

    barrier = pltpu.get_barrier_semaphore()
    for peer in (first, second, sibling):
        pl.semaphore_signal(barrier, inc=1, device_id=(peer, layer), device_id_type=MESH)
    for step in range(1, depth):
        pl.semaphore_signal(
            barrier, inc=1, device_id=(me, (layer + step) % depth), device_id_type=MESH
        )

    load_txt.wait()
    unit_txt, len_txt = normalize(raw_txt[...])
    col_in[layer] = jnp.concatenate([unit_txt[:, :half], unit_txt[:, half:]], axis=0).astype(
        BF16
    )
    load_img.wait()
    wide = raw_img[...].astype(F32)
    wide_img[...] = wide
    unit_all, _ = normalize(wide)
    img_buf[me] = unit_all.astype(BF16)

    pl.semaphore_wait(barrier, 2 + depth)

    started = []

    def push(src, dst, recv, device):
        copy = pltpu.make_async_remote_copy(
            src_ref=src,
            dst_ref=dst,
            send_sem=send_sem.at[len(started)],
            recv_sem=recv,
            device_id=device,
            device_id_type=MESH,
        )
        copy.start()
        started.append(copy)

    def part(buf, slot, chunk):
        return buf.at[slot, pl.ds(chunk * piece, piece)]

    def send(buf, slot, chunk, recv, *peers):
        for peer in peers:
            ref = part(buf, slot, chunk)
            push(ref, ref, recv.at[slot, chunk], (peer, layer))

    def landed(ref, recv):
        pltpu.make_async_remote_copy(
            src_ref=ref,
            dst_ref=ref,
            send_sem=send_sem.at[0],
            recv_sem=recv,
            device_id=(sibling, layer),
            device_id_type=MESH,
        ).wait_recv()

    def arrive(buf, slot, recv, *peers):
        for chunk in range(chunks):
            landed(part(buf, slot, chunk), recv.at[slot, chunk])
            send(buf, slot, chunk, recv, *peers)

    for step in range(1, depth):
        push(
            col_in.at[layer],
            col_in.at[layer],
            col_recv.at[layer],
            (me, (layer + step) % depth),
        )
    for chunk in range(chunks):
        send(img_buf, me, chunk, img_recv, first, second)
    for chunk in range(chunks):
        send(img_buf, me, chunk, img_recv, sibling)

    arrive(img_buf, first, img_recv, second, sibling)
    for step in range(1, depth):
        source = (layer + step) % depth
        landed(col_in.at[source], col_recv.at[source])
    pieces = []
    for z in range(depth):
        block = col_in[z].astype(F32)
        pieces.append(jnp.concatenate([block[:own], block[own:]], axis=1))
    txt_buf[me] = jnp.concatenate(pieces, axis=0).astype(BF16)
    for chunk in range(chunks):
        send(txt_buf, me, chunk, txt_recv, first, second)
    for chunk in range(chunks):
        send(txt_buf, me, chunk, txt_recv, sibling)

    arrive(img_buf, second, img_recv, sibling)
    arrive(img_buf, across, img_recv, sibling)
    arrive(txt_buf, first, txt_recv, second, sibling)
    for slot in (sibling, second + flip, first + flip, across + flip):
        arrive(img_buf, slot, img_recv)

    img_all = img_buf[...].reshape(total_rows, width)
    own_raw = wide_img[pl.ds(pl.multiple_of(layer * own, 8), own), :]
    own_img, len_img = normalize(own_raw)

    row_acc = jnp.zeros((8, total_rows), F32)
    row_sum = jnp.zeros((8, total_rows), F32)

    def absorb(start, count, row_acc, row_sum):
        block = txt_buf[pl.ds(start, count)].reshape(count * slot_rows, width)
        values = scaled_kernel(block, img_all)
        kt[pl.ds(start, count)] = values.reshape(count, slot_rows, total_rows)
        scale = 1.0 / jnp.sum(values, axis=1, keepdims=True)
        first_scale[pl.ds(start, count)] = scale.reshape(count, slot_rows, 1)
        return row_acc + fold_rows(values * scale), row_sum + fold_rows(values)

    arrive(txt_buf, sibling, txt_recv)
    row_acc, row_sum = absorb(me - core, 2, row_acc, row_sum)
    arrive(txt_buf, second, txt_recv, sibling)
    arrive(txt_buf, first + flip, txt_recv)
    row_acc, row_sum = absorb(first - core, 2, row_acc, row_sum)
    arrive(txt_buf, across, txt_recv, sibling)
    arrive(txt_buf, second + flip, txt_recv)
    row_acc, row_sum = absorb(second - core, 2, row_acc, row_sum)
    row_acc, row_sum = absorb(across, 1, row_acc, row_sum)
    arrive(txt_buf, across + flip, txt_recv)
    row_acc, row_sum = absorb(across + flip, 1, row_acc, row_sum)

    row_total = jnp.sum(row_sum, axis=0, keepdims=True)
    row_weight = 1.0 / jnp.sum(row_acc, axis=0, keepdims=True)
    previous = row_weight
    scales = []
    for step in range(1, ROUNDS):
        previous = row_weight
        row_acc = jnp.zeros((8, total_rows), F32)
        scales = []
        for slot in range(slots):
            scale = 1.0 / jnp.sum(kt[slot] * row_weight, axis=1, keepdims=True)
            row_acc += fold_rows(kt[slot] * scale)
            scales.append(scale)
        row_weight = 1.0 / jnp.sum(row_acc, axis=0, keepdims=True)

    keep = 1.0 - mix_weight
    lane = lax.broadcasted_iota(jnp.int32, (slot_rows, 128), 1)
    packed = []
    for slot in range(slots):
        last_cols = jnp.sum(kt[slot] * row_weight, axis=1, keepdims=True)
        weight = (keep + mix_weight * scales[slot] * last_cols) * first_scale[slot]
        packed.append(jnp.where(lane < 64, scales[slot], weight))
    packed = jnp.concatenate(packed, axis=0).T
    col_scale = packed[0:1]
    col_part = packed[64:65]

    at_row = lax.broadcasted_iota(jnp.int32, (own, total_rows), 0)
    at_col = lax.broadcasted_iota(jnp.int32, (own, total_rows), 1)

    def logit_grad(values, factor, place):
        eye = (at_col == at_row + place).astype(F32)
        return (0.5 * (values * factor - (2.0 * keep) * eye)).astype(BF16)

    values = scaled_kernel(unit_txt.astype(BF16), img_all)
    own_total = jnp.sum(values, axis=1, keepdims=True)
    own_scale = 1.0 / jnp.sum(values * previous, axis=1, keepdims=True)
    own_cols = jnp.sum(values * row_weight, axis=1, keepdims=True)
    own_part = (keep + mix_weight * own_scale * own_cols) / own_total
    factor = 1.0 / row_total + own_part - (2.0 * mix_weight) * (row_weight * own_scale)
    grad_logit = logit_grad(values, factor, layer * (slots * own) + me * own)
    g_txt = logit_scale * jnp.dot(grad_logit, img_all, preferred_element_type=F32)
    gtxt_ref[...] = project_back(g_txt, unit_txt, len_txt)

    txt_all = txt_buf[...].reshape(total_rows, width)
    values = scaled_kernel(own_img.astype(BF16), txt_all)
    own_total = jnp.sum(values, axis=1, keepdims=True)
    own_weight = 1.0 / jnp.sum(values * col_scale, axis=1, keepdims=True)
    group = me * depth + layer
    place = (group % slots) * slot_rows + (group // slots) * own
    factor = 1.0 / own_total + col_part - (2.0 * mix_weight) * (own_weight * col_scale)
    grad_logit = logit_grad(values, factor, place)
    g_img = logit_scale * jnp.dot(grad_logit, txt_all, preferred_element_type=F32)
    gimg_ref[...] = project_back(g_img, own_img, len_img)

    for copy in started:
        copy.wait_send()


def gathered(slots, depth, images, texts):
    slot_rows, width = images.shape
    own = texts.shape[0]
    total_rows = slots * slot_rows
    chunks = 2
    vmem = pl.BlockSpec(memory_space=pltpu.VMEM)
    anywhere = pl.BlockSpec(memory_space=pltpu.HBM)
    out = jax.ShapeDtypeStruct((own, width), F32)
    return pl.pallas_call(
        gathered_body,
        out_shape=(out, out),
        in_specs=[anywhere, anywhere],
        out_specs=(vmem, vmem),
        scratch_shapes=[
            pltpu.VMEM((slots, slot_rows, width), BF16),
            pltpu.VMEM((slots, slot_rows, width), BF16),
            pltpu.VMEM((depth, 2 * own, width // 2), BF16),
            pltpu.VMEM((slot_rows, width), F32),
            pltpu.VMEM((slot_rows, width), BF16),
            pltpu.VMEM((own, width), BF16),
            pltpu.VMEM((slots, slot_rows, total_rows), F32),
            pltpu.VMEM((slots, slot_rows, 1), F32),
            pltpu.SemaphoreType.DMA((depth - 1 + 14 * chunks,)),
            pltpu.SemaphoreType.DMA((slots, chunks)),
            pltpu.SemaphoreType.DMA((slots, chunks)),
            pltpu.SemaphoreType.DMA((depth,)),
            pltpu.SemaphoreType.DMA((2,)),
        ],
        compiler_params=pltpu.CompilerParams(
            collective_id=0, has_side_effects=True, vmem_limit_bytes=60 * 1024 * 1024
        ),
    )(images, texts)


def solution(mesh):
    placed = (P("img", None), P(("txt", "img"), None))
    slots, depth = mesh.shape["img"], mesh.shape["txt"]

    def body(images, texts):
        pairs = images.shape[0] * slots
        whole = slots == 8 and images.shape[0] % 32 == 0 and texts.shape[0] % 8 == 0
        if whole and pairs * pairs * 4 <= 4 * 1024 * 1024:
            return gathered(slots, depth, images, texts)
        return shards(images, texts)

    return jax.shard_map(
        body,
        mesh=mesh,
        in_specs=placed,
        out_specs=(P(("img", "txt"), None), P(("txt", "img"), None)),
        check_vma=False,
    )
```

```python
import jax
import jax.numpy as jnp
from jax import lax
from jax.experimental import pallas as pl
from jax.experimental.pallas import tpu as pltpu
from jax.sharding import PartitionSpec as P

ROUNDS = 3


logit_scale = 30.0
mix_weight = 0.5
norm_eps = 1e-06
highest = lax.Precision.HIGHEST


def normalize(values):
    wide = values.astype(jnp.float32)
    length = jnp.sqrt(jnp.sum(wide * wide, axis=1, keepdims=True) + norm_eps)
    return (wide / length, length)


def project_back(grad, unit, length):
    along = jnp.sum(unit * grad, axis=1, keepdims=True)
    return (grad - unit * along) / length


def shards(images, texts):
    own_rows = texts.shape[0]
    img_block = images.shape[0]
    img_index = lax.axis_index("img")
    txt_index = lax.axis_index("txt")
    unit_img, len_img = normalize(images)
    img_bf = unit_img.astype(jnp.bfloat16)
    unit_txt, len_txt = normalize(texts)
    txt_bf = lax.all_gather(unit_txt.astype(jnp.bfloat16), "img", axis=0, tiled=True)
    txt_block = txt_bf.shape[0]
    total = float(img_block * lax.axis_size("img"))
    scores = logit_scale * lax.dot_general(
        img_bf, txt_bf, (((1,), (1,)), ((), ())), preferred_element_type=jnp.float32
    )
    kernel = jnp.exp(scores - logit_scale)
    row_weight = jnp.ones((img_block,), jnp.float32)
    col_scale = jnp.ones((txt_block,), jnp.float32)
    col_total = col_scale
    row_total = row_weight
    last_cols = col_scale
    for step in range(ROUNDS + 1):
        col_part = jnp.dot(row_weight, kernel, precision=highest)
        col_sum = lax.psum(col_part, "img")
        if step == 0:
            col_total = col_sum
        if step == ROUNDS:
            last_cols = col_sum
        else:
            col_scale = 1.0 / (total * col_sum)
            row_part = jnp.dot(kernel, col_scale, precision=highest)
            if step == 0:
                stats = jnp.stack([row_part, jnp.sum(kernel, axis=1)])
            else:
                stats = row_part[None, :]
            summed = lax.psum(stats, "txt")
            if step == 0:
                row_total = summed[1]
            row_weight = 1.0 / (total * summed[0])
    col_weight = 1.0 - mix_weight + mix_weight * total * col_scale * last_cols
    img_ids = img_index * img_block + jnp.arange(img_block, dtype=jnp.int32)
    txt_ids = txt_index * txt_block + jnp.arange(txt_block, dtype=jnp.int32)
    eye = (img_ids[:, None] == txt_ids[None, :]).astype(jnp.float32)
    target = (1.0 - mix_weight) * eye + mix_weight * total * row_weight[
        :, None
    ] * kernel * col_scale[None, :]
    grad_logit = 0.5 * (
        kernel / row_total[:, None]
        + col_weight[None, :] * kernel / col_total[None, :]
        - 2.0 * target
    )
    grad_logit = grad_logit.astype(jnp.bfloat16)
    g_img = lax.psum_scatter(
        logit_scale * jnp.dot(grad_logit, txt_bf, preferred_element_type=jnp.float32),
        "txt",
        scatter_dimension=0,
        tiled=True,
    )
    g_txt = lax.psum_scatter(
        logit_scale
        * lax.dot_general(
            grad_logit, img_bf, (((0,), (0,)), ((), ())), preferred_element_type=jnp.float32
        ),
        "img",
        scatter_dimension=0,
        tiled=True,
    )
    own_unit = lax.dynamic_slice_in_dim(unit_img, txt_index * own_rows, own_rows, 0)
    own_len = lax.dynamic_slice_in_dim(len_img, txt_index * own_rows, own_rows, 0)
    grad_images = project_back(g_img, own_unit, own_len)
    grad_texts = project_back(g_txt, unit_txt, len_txt)
    return (grad_images, grad_texts)


MESH = pl.DeviceIdType.MESH
F32 = jnp.float32
BF16 = jnp.bfloat16


def nt_dot(left, right):
    return lax.dot_general(
        left, right, (((1,), (1,)), ((), ())), preferred_element_type=F32
    )


def scaled_kernel(left, right):
    return jnp.exp(logit_scale * nt_dot(left, right) - logit_scale)


def fold_rows(values):
    rows, cols = values.shape
    return jnp.sum(values.reshape(rows // 8, 8, cols), axis=0)


def gathered_body(
    images_ref,
    texts_ref,
    gimg_ref,
    gtxt_ref,
    img_buf,
    txt_buf,
    col_in,
    wide_img,
    raw_img,
    raw_txt,
    kt,
    first_scale,
    send_sem,
    img_recv,
    txt_recv,
    col_recv,
    load_sem,
):
    slots, slot_rows, width = img_buf.shape
    depth, own = col_in.shape[0], texts_ref.shape[0]
    half = width // 2
    total_rows = slots * slot_rows
    chunks = img_recv.shape[1]
    piece = slot_rows // chunks

    load_txt = pltpu.make_async_copy(texts_ref, raw_txt, load_sem.at[0])
    load_txt.start()
    load_img = pltpu.make_async_copy(images_ref, raw_img, load_sem.at[1])
    load_img.start()

    me = lax.axis_index("img")
    layer = lax.axis_index("txt")
    core = me % 2
    x = (me // 2) % 2
    y = me // 4
    first = (y + core * (1 - 2 * y)) * 4 + (x + (1 - core) * (1 - 2 * x)) * 2 + core
    second = (y + (1 - core) * (1 - 2 * y)) * 4 + (x + core * (1 - 2 * x)) * 2 + core
    across = (1 - y) * 4 + (1 - x) * 2 + core
    flip = 1 - 2 * core
    sibling = me + flip

    barrier = pltpu.get_barrier_semaphore()
    for peer in (first, second, sibling):
        pl.semaphore_signal(barrier, inc=1, device_id=(peer, layer), device_id_type=MESH)
    for step in range(1, depth):
        pl.semaphore_signal(
            barrier, inc=1, device_id=(me, (layer + step) % depth), device_id_type=MESH
        )

    load_txt.wait()
    unit_txt, len_txt = normalize(raw_txt[...])
    col_in[layer] = jnp.concatenate([unit_txt[:, :half], unit_txt[:, half:]], axis=0).astype(
        BF16
    )
    pl.semaphore_wait(barrier, 2 + depth)

    started = []

    def push(src, dst, recv, device):
        copy = pltpu.make_async_remote_copy(
            src_ref=src,
            dst_ref=dst,
            send_sem=send_sem.at[len(started)],
            recv_sem=recv,
            device_id=device,
            device_id_type=MESH,
        )
        copy.start()
        started.append(copy)

    def part(buf, slot, chunk):
        return buf.at[slot, pl.ds(chunk * piece, piece)]

    def send(buf, slot, chunk, recv, *peers):
        for peer in peers:
            ref = part(buf, slot, chunk)
            push(ref, ref, recv.at[slot, chunk], (peer, layer))

    def landed(ref, recv):
        pltpu.make_async_remote_copy(
            src_ref=ref,
            dst_ref=ref,
            send_sem=send_sem.at[0],
            recv_sem=recv,
            device_id=(sibling, layer),
            device_id_type=MESH,
        ).wait_recv()

    def arrive(buf, slot, recv, *peers):
        for chunk in range(chunks):
            landed(part(buf, slot, chunk), recv.at[slot, chunk])
            send(buf, slot, chunk, recv, *peers)

    for step in range(1, depth):
        push(
            col_in.at[layer],
            col_in.at[layer],
            col_recv.at[layer],
            (me, (layer + step) % depth),
        )
    load_img.wait()
    for chunk in range(chunks):
        rows = pl.ds(chunk * piece, piece)
        wide = raw_img[rows, :].astype(F32)
        wide_img[rows, :] = wide
        unit_part, _ = normalize(wide)
        img_buf[me, rows] = unit_part.astype(BF16)
        send(img_buf, me, chunk, img_recv, first, second, sibling)

    arrive(img_buf, first, img_recv, second, sibling)
    for step in range(1, depth):
        source = (layer + step) % depth
        landed(col_in.at[source], col_recv.at[source])
    pieces = []
    for z in range(depth):
        block = col_in[z].astype(F32)
        pieces.append(jnp.concatenate([block[:own], block[own:]], axis=1))
    txt_buf[me] = jnp.concatenate(pieces, axis=0).astype(BF16)
    for chunk in range(chunks):
        send(txt_buf, me, chunk, txt_recv, first, second)
    for chunk in range(chunks):
        send(txt_buf, me, chunk, txt_recv, sibling)

    arrive(img_buf, second, img_recv, sibling)
    arrive(img_buf, across, img_recv, sibling)
    arrive(txt_buf, first, txt_recv, second, sibling)
    for slot in (sibling, second + flip, first + flip, across + flip):
        arrive(img_buf, slot, img_recv)

    img_all = img_buf[...].reshape(total_rows, width)
    own_raw = wide_img[pl.ds(pl.multiple_of(layer * own, 8), own), :]
    own_img, len_img = normalize(own_raw)

    row_acc = jnp.zeros((8, total_rows), F32)
    row_sum = jnp.zeros((8, total_rows), F32)

    def absorb(start, count, row_acc, row_sum):
        block = txt_buf[pl.ds(start, count)].reshape(count * slot_rows, width)
        values = scaled_kernel(block, img_all)
        kt[pl.ds(start, count)] = values.reshape(count, slot_rows, total_rows)
        scale = 1.0 / jnp.sum(values, axis=1, keepdims=True)
        first_scale[pl.ds(start, count)] = scale.reshape(count, slot_rows, 1)
        return row_acc + fold_rows(values * scale), row_sum + fold_rows(values)

    arrive(txt_buf, sibling, txt_recv)
    row_acc, row_sum = absorb(me - core, 2, row_acc, row_sum)
    arrive(txt_buf, second, txt_recv, sibling)
    arrive(txt_buf, first + flip, txt_recv)
    row_acc, row_sum = absorb(first - core, 2, row_acc, row_sum)
    arrive(txt_buf, across, txt_recv, sibling)
    arrive(txt_buf, second + flip, txt_recv)
    row_acc, row_sum = absorb(second - core, 2, row_acc, row_sum)
    row_acc, row_sum = absorb(across, 1, row_acc, row_sum)
    arrive(txt_buf, across + flip, txt_recv)
    row_acc, row_sum = absorb(across + flip, 1, row_acc, row_sum)

    row_total = jnp.sum(row_sum, axis=0, keepdims=True)
    row_weight = 1.0 / jnp.sum(row_acc, axis=0, keepdims=True)
    previous = row_weight
    scales = []
    for step in range(1, ROUNDS):
        previous = row_weight
        row_acc = jnp.zeros((8, total_rows), F32)
        scales = []
        for slot in range(slots):
            scale = 1.0 / jnp.sum(kt[slot] * row_weight, axis=1, keepdims=True)
            row_acc += fold_rows(kt[slot] * scale)
            scales.append(scale)
        row_weight = 1.0 / jnp.sum(row_acc, axis=0, keepdims=True)

    keep = 1.0 - mix_weight
    lane = lax.broadcasted_iota(jnp.int32, (slot_rows, 128), 1)
    packed = []
    for slot in range(slots):
        last_cols = jnp.sum(kt[slot] * row_weight, axis=1, keepdims=True)
        weight = (keep + mix_weight * scales[slot] * last_cols) * first_scale[slot]
        packed.append(jnp.where(lane < 64, scales[slot], weight))
    packed = jnp.concatenate(packed, axis=0).T
    col_scale = packed[0:1]
    col_part = packed[64:65]

    at_row = lax.broadcasted_iota(jnp.int32, (own, total_rows), 0)
    at_col = lax.broadcasted_iota(jnp.int32, (own, total_rows), 1)

    def logit_grad(values, factor, place):
        eye = (at_col == at_row + place).astype(F32)
        return (0.5 * (values * factor - (2.0 * keep) * eye)).astype(BF16)

    values = scaled_kernel(unit_txt.astype(BF16), img_all)
    own_total = jnp.sum(values, axis=1, keepdims=True)
    own_scale = 1.0 / jnp.sum(values * previous, axis=1, keepdims=True)
    own_cols = jnp.sum(values * row_weight, axis=1, keepdims=True)
    own_part = (keep + mix_weight * own_scale * own_cols) / own_total
    factor = 1.0 / row_total + own_part - (2.0 * mix_weight) * (row_weight * own_scale)
    grad_logit = logit_grad(values, factor, layer * (slots * own) + me * own)
    g_txt = logit_scale * jnp.dot(grad_logit, img_all, preferred_element_type=F32)
    gtxt_ref[...] = project_back(g_txt, unit_txt, len_txt)

    txt_all = txt_buf[...].reshape(total_rows, width)
    values = scaled_kernel(own_img.astype(BF16), txt_all)
    own_total = jnp.sum(values, axis=1, keepdims=True)
    own_weight = 1.0 / jnp.sum(values * col_scale, axis=1, keepdims=True)
    group = me * depth + layer
    place = (group % slots) * slot_rows + (group // slots) * own
    factor = 1.0 / own_total + col_part - (2.0 * mix_weight) * (own_weight * col_scale)
    grad_logit = logit_grad(values, factor, place)
    g_img = logit_scale * jnp.dot(grad_logit, txt_all, preferred_element_type=F32)
    gimg_ref[...] = project_back(g_img, own_img, len_img)

    for copy in started:
        copy.wait_send()


def gathered(slots, depth, images, texts):
    slot_rows, width = images.shape
    own = texts.shape[0]
    total_rows = slots * slot_rows
    chunks = 2
    vmem = pl.BlockSpec(memory_space=pltpu.VMEM)
    anywhere = pl.BlockSpec(memory_space=pltpu.HBM)
    out = jax.ShapeDtypeStruct((own, width), F32)
    return pl.pallas_call(
        gathered_body,
        out_shape=(out, out),
        in_specs=[anywhere, anywhere],
        out_specs=(vmem, vmem),
        scratch_shapes=[
            pltpu.VMEM((slots, slot_rows, width), BF16),
            pltpu.VMEM((slots, slot_rows, width), BF16),
            pltpu.VMEM((depth, 2 * own, width // 2), BF16),
            pltpu.VMEM((slot_rows, width), F32),
            pltpu.VMEM((slot_rows, width), BF16),
            pltpu.VMEM((own, width), BF16),
            pltpu.VMEM((slots, slot_rows, total_rows), F32),
            pltpu.VMEM((slots, slot_rows, 1), F32),
            pltpu.SemaphoreType.DMA((depth - 1 + 14 * chunks,)),
            pltpu.SemaphoreType.DMA((slots, chunks)),
            pltpu.SemaphoreType.DMA((slots, chunks)),
            pltpu.SemaphoreType.DMA((depth,)),
            pltpu.SemaphoreType.DMA((2,)),
        ],
        compiler_params=pltpu.CompilerParams(
            collective_id=0, has_side_effects=True, vmem_limit_bytes=32 * 1024 * 1024
        ),
    )(*(pltpu.with_memory_space_constraint(array, pltpu.HBM) for array in (images, texts)))


def solution(mesh):
    placed = (P("img", None), P(("txt", "img"), None))
    slots, depth = mesh.shape["img"], mesh.shape["txt"]

    def body(images, texts):
        pairs = images.shape[0] * slots
        whole = slots == 8 and images.shape[0] % 32 == 0 and texts.shape[0] % 8 == 0
        if whole and pairs * pairs * 4 <= 4 * 1024 * 1024:
            return gathered(slots, depth, images, texts)
        return shards(images, texts)

    return jax.shard_map(
        body,
        mesh=mesh,
        in_specs=placed,
        out_specs=(P(("img", "txt"), None), P(("txt", "img"), None)),
        check_vma=False,
    )
```

```python
import jax
import jax.numpy as jnp
from jax import lax
from jax.experimental import pallas as pl
from jax.experimental.pallas import tpu as pltpu
from jax.sharding import PartitionSpec as P

ROUNDS = 3


logit_scale = 30.0
mix_weight = 0.5
norm_eps = 1e-06
highest = lax.Precision.HIGHEST


def normalize(values):
    wide = values.astype(jnp.float32)
    length = jnp.sqrt(jnp.sum(wide * wide, axis=1, keepdims=True) + norm_eps)
    return (wide / length, length)


def project_back(grad, unit, length):
    along = jnp.sum(unit * grad, axis=1, keepdims=True)
    return (grad - unit * along) / length


def shards(images, texts):
    own_rows = texts.shape[0]
    img_block = images.shape[0]
    img_index = lax.axis_index("img")
    txt_index = lax.axis_index("txt")
    unit_img, len_img = normalize(images)
    img_bf = unit_img.astype(jnp.bfloat16)
    unit_txt, len_txt = normalize(texts)
    txt_bf = lax.all_gather(unit_txt.astype(jnp.bfloat16), "img", axis=0, tiled=True)
    txt_block = txt_bf.shape[0]
    total = float(img_block * lax.axis_size("img"))
    scores = logit_scale * lax.dot_general(
        img_bf, txt_bf, (((1,), (1,)), ((), ())), preferred_element_type=jnp.float32
    )
    kernel = jnp.exp(scores - logit_scale)
    row_weight = jnp.ones((img_block,), jnp.float32)
    col_scale = jnp.ones((txt_block,), jnp.float32)
    col_total = col_scale
    row_total = row_weight
    last_cols = col_scale
    for step in range(ROUNDS + 1):
        col_part = jnp.dot(row_weight, kernel, precision=highest)
        col_sum = lax.psum(col_part, "img")
        if step == 0:
            col_total = col_sum
        if step == ROUNDS:
            last_cols = col_sum
        else:
            col_scale = 1.0 / (total * col_sum)
            row_part = jnp.dot(kernel, col_scale, precision=highest)
            if step == 0:
                stats = jnp.stack([row_part, jnp.sum(kernel, axis=1)])
            else:
                stats = row_part[None, :]
            summed = lax.psum(stats, "txt")
            if step == 0:
                row_total = summed[1]
            row_weight = 1.0 / (total * summed[0])
    col_weight = 1.0 - mix_weight + mix_weight * total * col_scale * last_cols
    img_ids = img_index * img_block + jnp.arange(img_block, dtype=jnp.int32)
    txt_ids = txt_index * txt_block + jnp.arange(txt_block, dtype=jnp.int32)
    eye = (img_ids[:, None] == txt_ids[None, :]).astype(jnp.float32)
    target = (1.0 - mix_weight) * eye + mix_weight * total * row_weight[
        :, None
    ] * kernel * col_scale[None, :]
    grad_logit = 0.5 * (
        kernel / row_total[:, None]
        + col_weight[None, :] * kernel / col_total[None, :]
        - 2.0 * target
    )
    grad_logit = grad_logit.astype(jnp.bfloat16)
    g_img = lax.psum_scatter(
        logit_scale * jnp.dot(grad_logit, txt_bf, preferred_element_type=jnp.float32),
        "txt",
        scatter_dimension=0,
        tiled=True,
    )
    g_txt = lax.psum_scatter(
        logit_scale
        * lax.dot_general(
            grad_logit, img_bf, (((0,), (0,)), ((), ())), preferred_element_type=jnp.float32
        ),
        "img",
        scatter_dimension=0,
        tiled=True,
    )
    own_unit = lax.dynamic_slice_in_dim(unit_img, txt_index * own_rows, own_rows, 0)
    own_len = lax.dynamic_slice_in_dim(len_img, txt_index * own_rows, own_rows, 0)
    grad_images = project_back(g_img, own_unit, own_len)
    grad_texts = project_back(g_txt, unit_txt, len_txt)
    return (grad_images, grad_texts)


MESH = pl.DeviceIdType.MESH
F32 = jnp.float32
BF16 = jnp.bfloat16


def nt_dot(left, right):
    return lax.dot_general(
        left, right, (((1,), (1,)), ((), ())), preferred_element_type=F32
    )


def scaled_kernel(left, right):
    return jnp.exp(logit_scale * nt_dot(left, right) - logit_scale)


def fold_rows(values):
    rows, cols = values.shape
    return jnp.sum(values.reshape(rows // 8, 8, cols), axis=0)


def gathered_body(
    images_ref,
    texts_ref,
    grad_ref,
    img_buf,
    txt_buf,
    txt_pack,
    wide_img,
    raw_img,
    raw_txt,
    kt,
    first_scale,
    send_sem,
    img_recv,
    txt_recv,
    load_sem,
):
    slots, slot_rows, width = img_buf.shape
    depth, own = txt_pack.shape[1], texts_ref.shape[0]
    half = width // 2
    total_rows = slots * slot_rows
    chunks = img_recv.shape[1]
    piece = slot_rows // chunks

    load_txt = pltpu.make_async_copy(texts_ref, raw_txt, load_sem.at[0])
    load_txt.start()
    load_img = pltpu.make_async_copy(images_ref, raw_img, load_sem.at[1])
    load_img.start()

    me = lax.axis_index("img")
    layer = lax.axis_index("txt")
    core = me % 2
    x = (me // 2) % 2
    y = me // 4
    first = (y + core * (1 - 2 * y)) * 4 + (x + (1 - core) * (1 - 2 * x)) * 2 + core
    second = (y + (1 - core) * (1 - 2 * y)) * 4 + (x + core * (1 - 2 * x)) * 2 + core
    across = (1 - y) * 4 + (1 - x) * 2 + core
    flip = 1 - 2 * core
    sibling = me + flip

    barrier = pltpu.get_barrier_semaphore()
    for peer in (first, second, sibling):
        pl.semaphore_signal(barrier, inc=1, device_id=(peer, layer), device_id_type=MESH)
    for step in range(1, depth):
        pl.semaphore_signal(
            barrier, inc=1, device_id=(me, (layer + step) % depth), device_id_type=MESH
        )

    load_txt.wait()
    unit_txt, len_txt = normalize(raw_txt[...])
    txt_pack[me, layer] = jnp.concatenate(
        [unit_txt[:, :half], unit_txt[:, half:]], axis=0
    ).astype(BF16)
    pl.semaphore_wait(barrier, 2 + depth)

    started = []

    def push(src, dst, recv, device):
        copy = pltpu.make_async_remote_copy(
            src_ref=src,
            dst_ref=dst,
            send_sem=send_sem.at[len(started)],
            recv_sem=recv,
            device_id=device,
            device_id_type=MESH,
        )
        copy.start()
        started.append(copy)

    def landed(ref, recv):
        pltpu.make_async_remote_copy(
            src_ref=ref,
            dst_ref=ref,
            send_sem=send_sem.at[0],
            recv_sem=recv,
            device_id=(sibling, layer),
            device_id_type=MESH,
        ).wait_recv()

    def send_img(slot, chunk, *peers):
        ref = img_buf.at[slot, pl.ds(chunk * piece, piece)]
        for peer in peers:
            push(ref, ref, img_recv.at[slot, chunk], (peer, layer))

    def arrive_img(slot, chunk, *peers):
        landed(img_buf.at[slot, pl.ds(chunk * piece, piece)], img_recv.at[slot, chunk])
        send_img(slot, chunk, *peers)

    def send_txt(slot, z, *peers):
        ref = txt_pack.at[slot, z]
        for peer in peers:
            push(ref, ref, txt_recv.at[slot, z], (peer, layer))

    def arrive_txt(slot, z, *peers):
        landed(txt_pack.at[slot, z], txt_recv.at[slot, z])
        send_txt(slot, z, *peers)

    layers = [layer] + [(layer + step) % depth for step in range(1, depth)]

    own_block = txt_pack.at[me, layer]
    for z in layers[1:]:
        push(own_block, own_block, txt_recv.at[me, layer], (me, z))
    send_txt(me, layer, first, second, sibling)

    load_img.wait()
    for chunk in range(chunks):
        rows = pl.ds(chunk * piece, piece)
        wide = raw_img[rows, :].astype(F32)
        wide_img[rows, :] = wide
        unit_part, _ = normalize(wide)
        img_buf[me, rows] = unit_part.astype(BF16)
        send_img(me, chunk, first, second, sibling)

    arrive_txt(first, layer, second, sibling)
    arrive_img(first, 0, second, sibling)
    for chunk in range(1, chunks):
        arrive_txt(me, layers[chunk], first, second, sibling)
        arrive_img(first, chunk, second, sibling)
    for z in layers[chunks:]:
        arrive_txt(me, z, first, second, sibling)
    for chunk in range(chunks):
        arrive_img(second, chunk, sibling)
    for z in layers[1:]:
        arrive_txt(first, z, second, sibling)
    for chunk in range(chunks):
        arrive_img(across, chunk, sibling)
    for slot in (sibling, second + flip, first + flip, across + flip):
        for chunk in range(chunks):
            arrive_img(slot, chunk)

    img_all = img_buf[...].reshape(total_rows, width)
    own_raw = wide_img[pl.ds(pl.multiple_of(layer * own, 8), own), :]
    own_img, len_img = normalize(own_raw)

    row_acc = jnp.zeros((8, total_rows), F32)
    row_sum = jnp.zeros((8, total_rows), F32)

    def unpack(slot):
        pieces = []
        for z in range(depth):
            block = txt_pack[slot, z].astype(F32)
            pieces.append(jnp.concatenate([block[:own], block[own:]], axis=1))
        txt_buf[slot] = jnp.concatenate(pieces, axis=0).astype(BF16)

    def absorb(start, count, row_acc, row_sum):
        for slot in range(count):
            unpack(start + slot)
        block = txt_buf[pl.ds(start, count)].reshape(count * slot_rows, width)
        values = scaled_kernel(block, img_all)
        kt[pl.ds(start, count)] = values.reshape(count, slot_rows, total_rows)
        scale = 1.0 / jnp.sum(values, axis=1, keepdims=True)
        first_scale[pl.ds(start, count)] = scale.reshape(count, slot_rows, 1)
        return row_acc + fold_rows(values * scale), row_sum + fold_rows(values)

    for z in layers:
        arrive_txt(sibling, z)
    row_acc, row_sum = absorb(me - core, 2, row_acc, row_sum)
    for z in layers:
        arrive_txt(second, z, sibling)
    for z in layers:
        arrive_txt(first + flip, z)
    row_acc, row_sum = absorb(first - core, 2, row_acc, row_sum)
    for z in layers:
        arrive_txt(across, z, sibling)
    for z in layers:
        arrive_txt(second + flip, z)
    row_acc, row_sum = absorb(second - core, 2, row_acc, row_sum)
    row_acc, row_sum = absorb(across, 1, row_acc, row_sum)
    for z in layers:
        arrive_txt(across + flip, z)
    row_acc, row_sum = absorb(across + flip, 1, row_acc, row_sum)

    row_total = jnp.sum(row_sum, axis=0, keepdims=True)
    row_weight = 1.0 / jnp.sum(row_acc, axis=0, keepdims=True)
    previous = row_weight
    scales = []
    for step in range(1, ROUNDS):
        previous = row_weight
        row_acc = jnp.zeros((8, total_rows), F32)
        scales = []
        for slot in range(slots):
            scale = 1.0 / jnp.sum(kt[slot] * row_weight, axis=1, keepdims=True)
            row_acc += fold_rows(kt[slot] * scale)
            scales.append(scale)
        row_weight = 1.0 / jnp.sum(row_acc, axis=0, keepdims=True)

    keep = 1.0 - mix_weight
    lane = lax.broadcasted_iota(jnp.int32, (slot_rows, 128), 1)
    packed = []
    for slot in range(slots):
        last_cols = jnp.sum(kt[slot] * row_weight, axis=1, keepdims=True)
        weight = (keep + mix_weight * scales[slot] * last_cols) * first_scale[slot]
        packed.append(jnp.where(lane < 64, scales[slot], weight))
    packed = jnp.concatenate(packed, axis=0).T
    col_scale = packed[0:1]
    col_part = packed[64:65]

    at_row = lax.broadcasted_iota(jnp.int32, (own, total_rows), 0)
    at_col = lax.broadcasted_iota(jnp.int32, (own, total_rows), 1)

    def logit_grad(values, factor, place):
        eye = (at_col == at_row + place).astype(F32)
        return (0.5 * (values * factor - (2.0 * keep) * eye)).astype(BF16)

    values = scaled_kernel(unit_txt.astype(BF16), img_all)
    own_total = jnp.sum(values, axis=1, keepdims=True)
    own_scale = 1.0 / jnp.sum(values * previous, axis=1, keepdims=True)
    own_cols = jnp.sum(values * row_weight, axis=1, keepdims=True)
    own_part = (keep + mix_weight * own_scale * own_cols) / own_total
    factor = 1.0 / row_total + own_part - (2.0 * mix_weight) * (row_weight * own_scale)
    grad_logit = logit_grad(values, factor, layer * (slots * own) + me * own)
    g_txt = logit_scale * jnp.dot(grad_logit, img_all, preferred_element_type=F32)
    grad_ref[own:] = project_back(g_txt, unit_txt, len_txt)

    txt_all = txt_buf[...].reshape(total_rows, width)
    values = scaled_kernel(own_img.astype(BF16), txt_all)
    own_total = jnp.sum(values, axis=1, keepdims=True)
    own_weight = 1.0 / jnp.sum(values * col_scale, axis=1, keepdims=True)
    group = me * depth + layer
    place = (group % slots) * slot_rows + (group // slots) * own
    factor = 1.0 / own_total + col_part - (2.0 * mix_weight) * (own_weight * col_scale)
    grad_logit = logit_grad(values, factor, place)
    g_img = logit_scale * jnp.dot(grad_logit, txt_all, preferred_element_type=F32)
    grad_ref[:own] = project_back(g_img, own_img, len_img)

    for copy in started:
        copy.wait_send()


def gathered(slots, depth, images, texts):
    slot_rows, width = images.shape
    own = texts.shape[0]
    total_rows = slots * slot_rows
    chunks = 2
    vmem = pl.BlockSpec(memory_space=pltpu.VMEM)
    anywhere = pl.BlockSpec(memory_space=pltpu.HBM)
    out = jax.ShapeDtypeStruct((2 * own, width), F32)
    packed = pl.pallas_call(
        gathered_body,
        out_shape=out,
        in_specs=[anywhere, anywhere],
        out_specs=vmem,
        scratch_shapes=[
            pltpu.VMEM((slots, slot_rows, width), BF16),
            pltpu.VMEM((slots, slot_rows, width), BF16),
            pltpu.VMEM((slots, depth, 2 * own, width // 2), BF16),
            pltpu.VMEM((slot_rows, width), F32),
            pltpu.VMEM((slot_rows, width), BF16),
            pltpu.VMEM((own, width), BF16),
            pltpu.VMEM((slots, slot_rows, total_rows), F32),
            pltpu.VMEM((slots, slot_rows, 1), F32),
            pltpu.SemaphoreType.DMA((depth - 1 + 7 * (depth + chunks),)),
            pltpu.SemaphoreType.DMA((slots, chunks)),
            pltpu.SemaphoreType.DMA((slots, depth)),
            pltpu.SemaphoreType.DMA((2,)),
        ],
        compiler_params=pltpu.CompilerParams(
            collective_id=0, has_side_effects=True, vmem_limit_bytes=32 * 1024 * 1024
        ),
    )(*(pltpu.with_memory_space_constraint(array, pltpu.HBM) for array in (images, texts)))
    return packed[:own], packed[own:]


def solution(mesh):
    placed = (P("img", None), P(("txt", "img"), None))
    slots, depth = mesh.shape["img"], mesh.shape["txt"]

    def body(images, texts):
        pairs = images.shape[0] * slots
        whole = slots == 8 and images.shape[0] % 32 == 0 and texts.shape[0] % 8 == 0
        if whole and pairs * pairs * 4 <= 4 * 1024 * 1024:
            return gathered(slots, depth, images, texts)
        return shards(images, texts)

    return jax.shard_map(
        body,
        mesh=mesh,
        in_specs=placed,
        out_specs=(P(("img", "txt"), None), P(("txt", "img"), None)),
        check_vma=False,
    )
```

```python
import jax
import jax.numpy as jnp
from jax import lax
from jax.experimental import pallas as pl
from jax.experimental.pallas import tpu as pltpu
from jax.sharding import PartitionSpec as P

ROUNDS = 3


logit_scale = 30.0
mix_weight = 0.5
norm_eps = 1e-06
highest = lax.Precision.HIGHEST


def normalize(values):
    wide = values.astype(jnp.float32)
    length = jnp.sqrt(jnp.sum(wide * wide, axis=1, keepdims=True) + norm_eps)
    return (wide / length, length)


def project_back(grad, unit, length):
    along = jnp.sum(unit * grad, axis=1, keepdims=True)
    return (grad - unit * along) / length


def shards(images, texts):
    own_rows = texts.shape[0]
    img_block = images.shape[0]
    img_index = lax.axis_index("img")
    txt_index = lax.axis_index("txt")
    unit_img, len_img = normalize(images)
    img_bf = unit_img.astype(jnp.bfloat16)
    unit_txt, len_txt = normalize(texts)
    txt_bf = lax.all_gather(unit_txt.astype(jnp.bfloat16), "img", axis=0, tiled=True)
    txt_block = txt_bf.shape[0]
    total = float(img_block * lax.axis_size("img"))
    scores = logit_scale * lax.dot_general(
        img_bf, txt_bf, (((1,), (1,)), ((), ())), preferred_element_type=jnp.float32
    )
    kernel = jnp.exp(scores - logit_scale)
    row_weight = jnp.ones((img_block,), jnp.float32)
    col_scale = jnp.ones((txt_block,), jnp.float32)
    col_total = col_scale
    row_total = row_weight
    last_cols = col_scale
    for step in range(ROUNDS + 1):
        col_part = jnp.dot(row_weight, kernel, precision=highest)
        col_sum = lax.psum(col_part, "img")
        if step == 0:
            col_total = col_sum
        if step == ROUNDS:
            last_cols = col_sum
        else:
            col_scale = 1.0 / (total * col_sum)
            row_part = jnp.dot(kernel, col_scale, precision=highest)
            if step == 0:
                stats = jnp.stack([row_part, jnp.sum(kernel, axis=1)])
            else:
                stats = row_part[None, :]
            summed = lax.psum(stats, "txt")
            if step == 0:
                row_total = summed[1]
            row_weight = 1.0 / (total * summed[0])
    col_weight = 1.0 - mix_weight + mix_weight * total * col_scale * last_cols
    img_ids = img_index * img_block + jnp.arange(img_block, dtype=jnp.int32)
    txt_ids = txt_index * txt_block + jnp.arange(txt_block, dtype=jnp.int32)
    eye = (img_ids[:, None] == txt_ids[None, :]).astype(jnp.float32)
    target = (1.0 - mix_weight) * eye + mix_weight * total * row_weight[
        :, None
    ] * kernel * col_scale[None, :]
    grad_logit = 0.5 * (
        kernel / row_total[:, None]
        + col_weight[None, :] * kernel / col_total[None, :]
        - 2.0 * target
    )
    grad_logit = grad_logit.astype(jnp.bfloat16)
    g_img = lax.psum_scatter(
        logit_scale * jnp.dot(grad_logit, txt_bf, preferred_element_type=jnp.float32),
        "txt",
        scatter_dimension=0,
        tiled=True,
    )
    g_txt = lax.psum_scatter(
        logit_scale
        * lax.dot_general(
            grad_logit, img_bf, (((0,), (0,)), ((), ())), preferred_element_type=jnp.float32
        ),
        "img",
        scatter_dimension=0,
        tiled=True,
    )
    own_unit = lax.dynamic_slice_in_dim(unit_img, txt_index * own_rows, own_rows, 0)
    own_len = lax.dynamic_slice_in_dim(len_img, txt_index * own_rows, own_rows, 0)
    grad_images = project_back(g_img, own_unit, own_len)
    grad_texts = project_back(g_txt, unit_txt, len_txt)
    return (grad_images, grad_texts)


MESH = pl.DeviceIdType.MESH
F32 = jnp.float32
BF16 = jnp.bfloat16


def nt_dot(left, right):
    return lax.dot_general(
        left, right, (((1,), (1,)), ((), ())), preferred_element_type=F32
    )


def scaled_kernel(left, right):
    return jnp.exp(logit_scale * nt_dot(left, right) - logit_scale)


def fold_rows(values):
    rows, cols = values.shape
    return jnp.sum(values.reshape(rows // 8, 8, cols), axis=0)


def gathered_body(
    images_ref,
    texts_ref,
    grad_ref,
    img_buf,
    txt_buf,
    col_in,
    wide_img,
    raw_img,
    raw_txt,
    kt,
    first_scale,
    send_sem,
    img_recv,
    txt_recv,
    col_recv,
    load_sem,
):
    slots, slot_rows, width = img_buf.shape
    depth, own = col_in.shape[0], texts_ref.shape[0]
    half = width // 2
    total_rows = slots * slot_rows
    chunks = img_recv.shape[1]
    piece = slot_rows // chunks

    load_txt = pltpu.make_async_copy(texts_ref, raw_txt, load_sem.at[0])
    load_txt.start()
    load_img = pltpu.make_async_copy(images_ref, raw_img, load_sem.at[1])
    load_img.start()

    me = lax.axis_index("img")
    layer = lax.axis_index("txt")
    core = me % 2
    x = (me // 2) % 2
    y = me // 4
    first = (y + core * (1 - 2 * y)) * 4 + (x + (1 - core) * (1 - 2 * x)) * 2 + core
    second = (y + (1 - core) * (1 - 2 * y)) * 4 + (x + core * (1 - 2 * x)) * 2 + core
    across = (1 - y) * 4 + (1 - x) * 2 + core
    flip = 1 - 2 * core
    sibling = me + flip

    barrier = pltpu.get_barrier_semaphore()
    for peer in (first, second, sibling):
        pl.semaphore_signal(barrier, inc=1, device_id=(peer, layer), device_id_type=MESH)
    for step in range(1, depth):
        pl.semaphore_signal(
            barrier, inc=1, device_id=(me, (layer + step) % depth), device_id_type=MESH
        )

    load_txt.wait()
    unit_txt, len_txt = normalize(raw_txt[...])
    col_in[layer] = jnp.concatenate([unit_txt[:, :half], unit_txt[:, half:]], axis=0).astype(
        BF16
    )
    pl.semaphore_wait(barrier, 2 + depth)

    started = []

    def push(src, dst, recv, device):
        copy = pltpu.make_async_remote_copy(
            src_ref=src,
            dst_ref=dst,
            send_sem=send_sem.at[len(started)],
            recv_sem=recv,
            device_id=device,
            device_id_type=MESH,
        )
        copy.start()
        started.append(copy)

    def part(buf, slot, chunk):
        return buf.at[slot, pl.ds(chunk * piece, piece)]

    def send(buf, slot, chunk, recv, *peers):
        for peer in peers:
            ref = part(buf, slot, chunk)
            push(ref, ref, recv.at[slot, chunk], (peer, layer))

    def landed(ref, recv):
        pltpu.make_async_remote_copy(
            src_ref=ref,
            dst_ref=ref,
            send_sem=send_sem.at[0],
            recv_sem=recv,
            device_id=(sibling, layer),
            device_id_type=MESH,
        ).wait_recv()

    def arrive(buf, slot, recv, *peers):
        for chunk in range(chunks):
            landed(part(buf, slot, chunk), recv.at[slot, chunk])
            send(buf, slot, chunk, recv, *peers)

    for step in range(1, depth):
        push(
            col_in.at[layer],
            col_in.at[layer],
            col_recv.at[layer],
            (me, (layer + step) % depth),
        )
    load_img.wait()
    for chunk in range(chunks):
        rows = pl.ds(chunk * piece, piece)
        wide = raw_img[rows, :].astype(F32)
        wide_img[rows, :] = wide
        unit_part, _ = normalize(wide)
        img_buf[me, rows] = unit_part.astype(BF16)
        send(img_buf, me, chunk, img_recv, first, second, sibling)

    arrive(img_buf, first, img_recv, second, sibling)
    for step in range(1, depth):
        source = (layer + step) % depth
        landed(col_in.at[source], col_recv.at[source])
    pieces = []
    for z in range(depth):
        block = col_in[z].astype(F32)
        pieces.append(jnp.concatenate([block[:own], block[own:]], axis=1))
    txt_buf[me] = jnp.concatenate(pieces, axis=0).astype(BF16)
    for chunk in range(chunks):
        send(txt_buf, me, chunk, txt_recv, first, second)
    for chunk in range(chunks):
        send(txt_buf, me, chunk, txt_recv, sibling)

    arrive(img_buf, second, img_recv, sibling)
    arrive(img_buf, across, img_recv, sibling)
    arrive(txt_buf, first, txt_recv, second, sibling)
    for slot in (sibling, second + flip, first + flip, across + flip):
        arrive(img_buf, slot, img_recv)

    img_all = img_buf[...].reshape(total_rows, width)
    own_raw = wide_img[pl.ds(pl.multiple_of(layer * own, 8), own), :]
    own_img, len_img = normalize(own_raw)

    row_acc = jnp.zeros((8, total_rows), F32)
    row_sum = jnp.zeros((8, total_rows), F32)

    def absorb(start, count, row_acc, row_sum):
        block = txt_buf[pl.ds(start, count)].reshape(count * slot_rows, width)
        values = scaled_kernel(block, img_all)
        kt[pl.ds(start, count)] = values.reshape(count, slot_rows, total_rows)
        scale = 1.0 / jnp.sum(values, axis=1, keepdims=True)
        first_scale[pl.ds(start, count)] = scale.reshape(count, slot_rows, 1)
        return row_acc + fold_rows(values * scale), row_sum + fold_rows(values)

    arrive(txt_buf, sibling, txt_recv)
    row_acc, row_sum = absorb(me - core, 2, row_acc, row_sum)
    arrive(txt_buf, second, txt_recv, sibling)
    arrive(txt_buf, first + flip, txt_recv)
    row_acc, row_sum = absorb(first - core, 2, row_acc, row_sum)
    arrive(txt_buf, across, txt_recv, sibling)
    arrive(txt_buf, second + flip, txt_recv)
    row_acc, row_sum = absorb(second - core, 2, row_acc, row_sum)
    row_acc, row_sum = absorb(across, 1, row_acc, row_sum)
    arrive(txt_buf, across + flip, txt_recv)
    row_acc, row_sum = absorb(across + flip, 1, row_acc, row_sum)

    row_total = jnp.sum(row_sum, axis=0, keepdims=True)
    row_weight = 1.0 / jnp.sum(row_acc, axis=0, keepdims=True)
    previous = row_weight
    scales = []
    for step in range(1, ROUNDS):
        previous = row_weight
        row_acc = jnp.zeros((8, total_rows), F32)
        scales = []
        for slot in range(slots):
            scale = 1.0 / jnp.sum(kt[slot] * row_weight, axis=1, keepdims=True)
            row_acc += fold_rows(kt[slot] * scale)
            scales.append(scale)
        row_weight = 1.0 / jnp.sum(row_acc, axis=0, keepdims=True)

    keep = 1.0 - mix_weight
    lane = lax.broadcasted_iota(jnp.int32, (slot_rows, 128), 1)
    packed = []
    for slot in range(slots):
        last_cols = jnp.sum(kt[slot] * row_weight, axis=1, keepdims=True)
        weight = (keep + mix_weight * scales[slot] * last_cols) * first_scale[slot]
        packed.append(jnp.where(lane < 64, scales[slot], weight))
    packed = jnp.concatenate(packed, axis=0).T
    col_scale = packed[0:1]
    col_part = packed[64:65]

    at_row = lax.broadcasted_iota(jnp.int32, (own, total_rows), 0)
    at_col = lax.broadcasted_iota(jnp.int32, (own, total_rows), 1)

    def logit_grad(values, factor, place):
        eye = (at_col == at_row + place).astype(F32)
        return (0.5 * (values * factor - (2.0 * keep) * eye)).astype(BF16)

    values = scaled_kernel(unit_txt.astype(BF16), img_all)
    own_total = jnp.sum(values, axis=1, keepdims=True)
    own_scale = 1.0 / jnp.sum(values * previous, axis=1, keepdims=True)
    own_cols = jnp.sum(values * row_weight, axis=1, keepdims=True)
    own_part = (keep + mix_weight * own_scale * own_cols) / own_total
    factor = 1.0 / row_total + own_part - (2.0 * mix_weight) * (row_weight * own_scale)
    grad_logit = logit_grad(values, factor, layer * (slots * own) + me * own)
    g_txt = logit_scale * jnp.dot(grad_logit, img_all, preferred_element_type=F32)
    grad_ref[own:] = project_back(g_txt, unit_txt, len_txt)

    txt_all = txt_buf[...].reshape(total_rows, width)
    values = scaled_kernel(own_img.astype(BF16), txt_all)
    own_total = jnp.sum(values, axis=1, keepdims=True)
    own_weight = 1.0 / jnp.sum(values * col_scale, axis=1, keepdims=True)
    group = me * depth + layer
    place = (group % slots) * slot_rows + (group // slots) * own
    factor = 1.0 / own_total + col_part - (2.0 * mix_weight) * (own_weight * col_scale)
    grad_logit = logit_grad(values, factor, place)
    g_img = logit_scale * jnp.dot(grad_logit, txt_all, preferred_element_type=F32)
    grad_ref[:own] = project_back(g_img, own_img, len_img)

    for copy in started:
        copy.wait_send()


def gathered(slots, depth, images, texts):
    slot_rows, width = images.shape
    own = texts.shape[0]
    total_rows = slots * slot_rows
    chunks = 1
    vmem = pl.BlockSpec(memory_space=pltpu.VMEM)
    anywhere = pl.BlockSpec(memory_space=pltpu.HBM)
    out = jax.ShapeDtypeStruct((2 * own, width), F32)
    packed = pl.pallas_call(
        gathered_body,
        out_shape=out,
        in_specs=[anywhere, anywhere],
        out_specs=vmem,
        scratch_shapes=[
            pltpu.VMEM((slots, slot_rows, width), BF16),
            pltpu.VMEM((slots, slot_rows, width), BF16),
            pltpu.VMEM((depth, 2 * own, width // 2), BF16),
            pltpu.VMEM((slot_rows, width), F32),
            pltpu.VMEM((slot_rows, width), BF16),
            pltpu.VMEM((own, width), BF16),
            pltpu.VMEM((slots, slot_rows, total_rows), F32),
            pltpu.VMEM((slots, slot_rows, 1), F32),
            pltpu.SemaphoreType.DMA((depth - 1 + 14 * chunks,)),
            pltpu.SemaphoreType.DMA((slots, chunks)),
            pltpu.SemaphoreType.DMA((slots, chunks)),
            pltpu.SemaphoreType.DMA((depth,)),
            pltpu.SemaphoreType.DMA((2,)),
        ],
        compiler_params=pltpu.CompilerParams(
            collective_id=0, has_side_effects=True, vmem_limit_bytes=32 * 1024 * 1024
        ),
    )(*(pltpu.with_memory_space_constraint(array, pltpu.HBM) for array in (images, texts)))
    return packed[:own], packed[own:]


def solution(mesh):
    placed = (P("img", None), P(("txt", "img"), None))
    slots, depth = mesh.shape["img"], mesh.shape["txt"]

    def body(images, texts):
        pairs = images.shape[0] * slots
        whole = slots == 8 and images.shape[0] % 32 == 0 and texts.shape[0] % 8 == 0
        if whole and pairs * pairs * 4 <= 4 * 1024 * 1024:
            return gathered(slots, depth, images, texts)
        return shards(images, texts)

    return jax.shard_map(
        body,
        mesh=mesh,
        in_specs=placed,
        out_specs=(P(("img", "txt"), None), P(("txt", "img"), None)),
        check_vma=False,
    )
```

```python
import jax
import jax.numpy as jnp
from jax import lax
from jax.experimental import pallas as pl
from jax.experimental.pallas import tpu as pltpu
from jax.sharding import PartitionSpec as P

ROUNDS = 3


logit_scale = 30.0
mix_weight = 0.5
norm_eps = 1e-06
highest = lax.Precision.HIGHEST


def normalize(values):
    wide = values.astype(jnp.float32)
    length = jnp.sqrt(jnp.sum(wide * wide, axis=1, keepdims=True) + norm_eps)
    return (wide / length, length)


def project_back(grad, unit, length):
    along = jnp.sum(unit * grad, axis=1, keepdims=True)
    return (grad - unit * along) / length


def shards(images, texts):
    own_rows = texts.shape[0]
    img_block = images.shape[0]
    img_index = lax.axis_index("img")
    txt_index = lax.axis_index("txt")
    unit_img, len_img = normalize(images)
    img_bf = unit_img.astype(jnp.bfloat16)
    unit_txt, len_txt = normalize(texts)
    txt_bf = lax.all_gather(unit_txt.astype(jnp.bfloat16), "img", axis=0, tiled=True)
    txt_block = txt_bf.shape[0]
    total = float(img_block * lax.axis_size("img"))
    scores = logit_scale * lax.dot_general(
        img_bf, txt_bf, (((1,), (1,)), ((), ())), preferred_element_type=jnp.float32
    )
    kernel = jnp.exp(scores - logit_scale)
    row_weight = jnp.ones((img_block,), jnp.float32)
    col_scale = jnp.ones((txt_block,), jnp.float32)
    col_total = col_scale
    row_total = row_weight
    last_cols = col_scale
    for step in range(ROUNDS + 1):
        col_part = jnp.dot(row_weight, kernel, precision=highest)
        col_sum = lax.psum(col_part, "img")
        if step == 0:
            col_total = col_sum
        if step == ROUNDS:
            last_cols = col_sum
        else:
            col_scale = 1.0 / (total * col_sum)
            row_part = jnp.dot(kernel, col_scale, precision=highest)
            if step == 0:
                stats = jnp.stack([row_part, jnp.sum(kernel, axis=1)])
            else:
                stats = row_part[None, :]
            summed = lax.psum(stats, "txt")
            if step == 0:
                row_total = summed[1]
            row_weight = 1.0 / (total * summed[0])
    col_weight = 1.0 - mix_weight + mix_weight * total * col_scale * last_cols
    img_ids = img_index * img_block + jnp.arange(img_block, dtype=jnp.int32)
    txt_ids = txt_index * txt_block + jnp.arange(txt_block, dtype=jnp.int32)
    eye = (img_ids[:, None] == txt_ids[None, :]).astype(jnp.float32)
    target = (1.0 - mix_weight) * eye + mix_weight * total * row_weight[
        :, None
    ] * kernel * col_scale[None, :]
    grad_logit = 0.5 * (
        kernel / row_total[:, None]
        + col_weight[None, :] * kernel / col_total[None, :]
        - 2.0 * target
    )
    grad_logit = grad_logit.astype(jnp.bfloat16)
    g_img = lax.psum_scatter(
        logit_scale * jnp.dot(grad_logit, txt_bf, preferred_element_type=jnp.float32),
        "txt",
        scatter_dimension=0,
        tiled=True,
    )
    g_txt = lax.psum_scatter(
        logit_scale
        * lax.dot_general(
            grad_logit, img_bf, (((0,), (0,)), ((), ())), preferred_element_type=jnp.float32
        ),
        "img",
        scatter_dimension=0,
        tiled=True,
    )
    own_unit = lax.dynamic_slice_in_dim(unit_img, txt_index * own_rows, own_rows, 0)
    own_len = lax.dynamic_slice_in_dim(len_img, txt_index * own_rows, own_rows, 0)
    grad_images = project_back(g_img, own_unit, own_len)
    grad_texts = project_back(g_txt, unit_txt, len_txt)
    return (grad_images, grad_texts)


MESH = pl.DeviceIdType.MESH
F32 = jnp.float32
BF16 = jnp.bfloat16


def scaled_kernel(left, right):
    scores = jnp.dot(left, right, preferred_element_type=F32)
    return jnp.exp(logit_scale * scores - logit_scale)


def fold_rows(values):
    rows, cols = values.shape
    return jnp.sum(values.reshape(rows // 8, 8, cols), axis=0)


def gathered_body(
    images_ref,
    texts_ref,
    grad_ref,
    img_buf,
    txt_buf,
    col_in,
    wide_img,
    raw_img,
    raw_txt,
    kt,
    first_scale,
    img_turned,
    own_turned,
    own_scores,
    send_sem,
    img_recv,
    txt_recv,
    col_recv,
    load_sem,
):
    slots, slot_rows, width = img_buf.shape
    depth, own = col_in.shape[0], texts_ref.shape[0]
    half = width // 2
    total_rows = slots * slot_rows
    chunks = img_recv.shape[1]
    piece = slot_rows // chunks

    load_txt = pltpu.make_async_copy(texts_ref, raw_txt, load_sem.at[0])
    load_txt.start()
    load_img = pltpu.make_async_copy(images_ref, raw_img, load_sem.at[1])
    load_img.start()

    me = lax.axis_index("img")
    layer = lax.axis_index("txt")
    core = me % 2
    x = (me // 2) % 2
    y = me // 4
    first = (y + core * (1 - 2 * y)) * 4 + (x + (1 - core) * (1 - 2 * x)) * 2 + core
    second = (y + (1 - core) * (1 - 2 * y)) * 4 + (x + core * (1 - 2 * x)) * 2 + core
    across = (1 - y) * 4 + (1 - x) * 2 + core
    flip = 1 - 2 * core
    sibling = me + flip

    barrier = pltpu.get_barrier_semaphore()
    for peer in (first, second, sibling):
        pl.semaphore_signal(barrier, inc=1, device_id=(peer, layer), device_id_type=MESH)
    for step in range(1, depth):
        pl.semaphore_signal(
            barrier, inc=1, device_id=(me, (layer + step) % depth), device_id_type=MESH
        )

    load_txt.wait()
    unit_txt, len_txt = normalize(raw_txt[...])
    col_in[layer] = jnp.concatenate([unit_txt[:, :half], unit_txt[:, half:]], axis=0).astype(
        BF16
    )
    pl.semaphore_wait(barrier, 2 + depth)

    started = []

    def push(src, dst, recv, device):
        copy = pltpu.make_async_remote_copy(
            src_ref=src,
            dst_ref=dst,
            send_sem=send_sem.at[len(started)],
            recv_sem=recv,
            device_id=device,
            device_id_type=MESH,
        )
        copy.start()
        started.append(copy)

    def part(buf, slot, chunk):
        return buf.at[slot, pl.ds(chunk * piece, piece)]

    def send(buf, slot, chunk, recv, *peers):
        for peer in peers:
            ref = part(buf, slot, chunk)
            push(ref, ref, recv.at[slot, chunk], (peer, layer))

    def landed(ref, recv):
        pltpu.make_async_remote_copy(
            src_ref=ref,
            dst_ref=ref,
            send_sem=send_sem.at[0],
            recv_sem=recv,
            device_id=(sibling, layer),
            device_id_type=MESH,
        ).wait_recv()

    def arrive(buf, slot, recv, *peers):
        for chunk in range(chunks):
            landed(part(buf, slot, chunk), recv.at[slot, chunk])
            send(buf, slot, chunk, recv, *peers)

    for step in range(1, depth):
        push(
            col_in.at[layer],
            col_in.at[layer],
            col_recv.at[layer],
            (me, (layer + step) % depth),
        )
    load_img.wait()
    for chunk in range(chunks):
        rows = pl.ds(chunk * piece, piece)
        wide = raw_img[rows, :].astype(F32)
        wide_img[rows, :] = wide
        unit_part, _ = normalize(wide)
        img_buf[me, rows] = unit_part.astype(BF16)
        send(img_buf, me, chunk, img_recv, first, second, sibling)

    arrive(img_buf, first, img_recv, second, sibling)
    for step in range(1, depth):
        source = (layer + step) % depth
        landed(col_in.at[source], col_recv.at[source])
    pieces = []
    for z in range(depth):
        block = col_in[z].astype(F32)
        pieces.append(jnp.concatenate([block[:own], block[own:]], axis=1))
    txt_buf[me] = jnp.concatenate(pieces, axis=0).astype(BF16)
    for chunk in range(chunks):
        send(txt_buf, me, chunk, txt_recv, first, second)
    for chunk in range(chunks):
        send(txt_buf, me, chunk, txt_recv, sibling)

    arrive(img_buf, second, img_recv, sibling)
    arrive(img_buf, across, img_recv, sibling)
    arrive(txt_buf, first, txt_recv, second, sibling)
    for slot in (sibling, second + flip, first + flip, across + flip):
        arrive(img_buf, slot, img_recv)

    img_all = img_buf[...].reshape(total_rows, width)
    own_raw = wide_img[pl.ds(pl.multiple_of(layer * own, 8), own), :]
    own_img, len_img = normalize(own_raw)
    img_turned[...] = img_all.T
    padded = jnp.concatenate([own_img, jnp.zeros((128 - own, width), F32)], axis=0)
    own_turned[...] = padded.T.astype(BF16)

    row_acc = jnp.zeros((8, total_rows), F32)
    row_sum = jnp.zeros((8, total_rows), F32)

    def absorb(start, count, row_acc, row_sum):
        block = txt_buf[pl.ds(start, count)].reshape(count * slot_rows, width)
        values = scaled_kernel(block, img_turned[...])
        own_scores[pl.ds(start, count)] = jnp.dot(
            block, own_turned[...], preferred_element_type=F32
        ).reshape(count, slot_rows, 128)
        kt[pl.ds(start, count)] = values.reshape(count, slot_rows, total_rows)
        scale = 1.0 / jnp.sum(values, axis=1, keepdims=True)
        first_scale[pl.ds(start, count)] = scale.reshape(count, slot_rows, 1)
        return row_acc + fold_rows(values * scale), row_sum + fold_rows(values)

    arrive(txt_buf, sibling, txt_recv)
    row_acc, row_sum = absorb(me - core, 2, row_acc, row_sum)
    arrive(txt_buf, second, txt_recv, sibling)
    arrive(txt_buf, first + flip, txt_recv)
    row_acc, row_sum = absorb(first - core, 2, row_acc, row_sum)
    arrive(txt_buf, across, txt_recv, sibling)
    arrive(txt_buf, second + flip, txt_recv)
    row_acc, row_sum = absorb(second - core, 2, row_acc, row_sum)
    row_acc, row_sum = absorb(across, 1, row_acc, row_sum)
    arrive(txt_buf, across + flip, txt_recv)
    row_acc, row_sum = absorb(across + flip, 1, row_acc, row_sum)

    row_total = jnp.sum(row_sum, axis=0, keepdims=True)
    row_weight = 1.0 / jnp.sum(row_acc, axis=0, keepdims=True)
    previous = row_weight
    scales = []
    for step in range(1, ROUNDS):
        previous = row_weight
        row_acc = jnp.zeros((8, total_rows), F32)
        scales = []
        for slot in range(slots):
            scale = 1.0 / jnp.sum(kt[slot] * row_weight, axis=1, keepdims=True)
            row_acc += fold_rows(kt[slot] * scale)
            scales.append(scale)
        row_weight = 1.0 / jnp.sum(row_acc, axis=0, keepdims=True)

    keep = 1.0 - mix_weight
    lane = lax.broadcasted_iota(jnp.int32, (slot_rows, 128), 1)
    packed = []
    for slot in range(slots):
        last_cols = jnp.sum(kt[slot] * row_weight, axis=1, keepdims=True)
        weight = (keep + mix_weight * scales[slot] * last_cols) * first_scale[slot]
        packed.append(jnp.where(lane < 64, scales[slot], weight))
    packed = jnp.concatenate(packed, axis=0).T
    col_scale = packed[0:1]
    col_part = packed[64:65]

    at_row = lax.broadcasted_iota(jnp.int32, (own, total_rows), 0)
    at_col = lax.broadcasted_iota(jnp.int32, (own, total_rows), 1)

    def logit_grad(values, factor, place):
        eye = (at_col == at_row + place).astype(F32)
        return (0.5 * (values * factor - (2.0 * keep) * eye)).astype(BF16)

    values = scaled_kernel(unit_txt.astype(BF16), img_turned[...])
    own_total = jnp.sum(values, axis=1, keepdims=True)
    own_scale = 1.0 / jnp.sum(values * previous, axis=1, keepdims=True)
    own_cols = jnp.sum(values * row_weight, axis=1, keepdims=True)
    own_part = (keep + mix_weight * own_scale * own_cols) / own_total
    factor = 1.0 / row_total + own_part - (2.0 * mix_weight) * (row_weight * own_scale)
    grad_logit = logit_grad(values, factor, layer * (slots * own) + me * own)
    g_txt = logit_scale * jnp.dot(grad_logit, img_all, preferred_element_type=F32)
    grad_ref[own:] = project_back(g_txt, unit_txt, len_txt)

    txt_all = txt_buf[...].reshape(total_rows, width)
    scores = own_scores[...].reshape(total_rows, 128).T[:own]
    values = jnp.exp(logit_scale * scores - logit_scale)
    own_total = jnp.sum(values, axis=1, keepdims=True)
    own_weight = 1.0 / jnp.sum(values * col_scale, axis=1, keepdims=True)
    group = me * depth + layer
    place = (group % slots) * slot_rows + (group // slots) * own
    factor = 1.0 / own_total + col_part - (2.0 * mix_weight) * (own_weight * col_scale)
    grad_logit = logit_grad(values, factor, place)
    g_img = logit_scale * jnp.dot(grad_logit, txt_all, preferred_element_type=F32)
    grad_ref[:own] = project_back(g_img, own_img, len_img)

    for copy in started:
        copy.wait_send()


def gathered(slots, depth, images, texts):
    slot_rows, width = images.shape
    own = texts.shape[0]
    total_rows = slots * slot_rows
    chunks = 1
    vmem = pl.BlockSpec(memory_space=pltpu.VMEM)
    anywhere = pl.BlockSpec(memory_space=pltpu.HBM)
    out = jax.ShapeDtypeStruct((2 * own, width), F32)
    packed = pl.pallas_call(
        gathered_body,
        out_shape=out,
        in_specs=[anywhere, anywhere],
        out_specs=vmem,
        scratch_shapes=[
            pltpu.VMEM((slots, slot_rows, width), BF16),
            pltpu.VMEM((slots, slot_rows, width), BF16),
            pltpu.VMEM((depth, 2 * own, width // 2), BF16),
            pltpu.VMEM((slot_rows, width), F32),
            pltpu.VMEM((slot_rows, width), BF16),
            pltpu.VMEM((own, width), BF16),
            pltpu.VMEM((slots, slot_rows, total_rows), F32),
            pltpu.VMEM((slots, slot_rows, 1), F32),
            pltpu.VMEM((width, total_rows), BF16),
            pltpu.VMEM((width, 128), BF16),
            pltpu.VMEM((slots, slot_rows, 128), F32),
            pltpu.SemaphoreType.DMA((depth - 1 + 14 * chunks,)),
            pltpu.SemaphoreType.DMA((slots, chunks)),
            pltpu.SemaphoreType.DMA((slots, chunks)),
            pltpu.SemaphoreType.DMA((depth,)),
            pltpu.SemaphoreType.DMA((2,)),
        ],
        compiler_params=pltpu.CompilerParams(
            collective_id=0, has_side_effects=True, vmem_limit_bytes=32 * 1024 * 1024
        ),
    )(*(pltpu.with_memory_space_constraint(array, pltpu.HBM) for array in (images, texts)))
    return packed[:own], packed[own:]


def solution(mesh):
    placed = (P("img", None), P(("txt", "img"), None))
    slots, depth = mesh.shape["img"], mesh.shape["txt"]

    def body(images, texts):
        pairs = images.shape[0] * slots
        whole = slots == 8 and images.shape[0] % 32 == 0 and texts.shape[0] % 8 == 0
        if whole and pairs * pairs * 4 <= 4 * 1024 * 1024:
            return gathered(slots, depth, images, texts)
        return shards(images, texts)

    return jax.shard_map(
        body,
        mesh=mesh,
        in_specs=placed,
        out_specs=(P(("img", "txt"), None), P(("txt", "img"), None)),
        check_vma=False,
    )
```

```python
import jax
import jax.numpy as jnp
from jax import lax
from jax.experimental import pallas as pl
from jax.experimental.pallas import tpu as pltpu
from jax.sharding import PartitionSpec as P

ROUNDS = 3


logit_scale = 30.0
mix_weight = 0.5
norm_eps = 1e-06
highest = lax.Precision.HIGHEST


def normalize(values):
    wide = values.astype(jnp.float32)
    length = jnp.sqrt(jnp.sum(wide * wide, axis=1, keepdims=True) + norm_eps)
    return (wide / length, length)


def project_back(grad, unit, length):
    along = jnp.sum(unit * grad, axis=1, keepdims=True)
    return (grad - unit * along) / length


def shards(images, texts):
    own_rows = texts.shape[0]
    img_block = images.shape[0]
    img_index = lax.axis_index("img")
    txt_index = lax.axis_index("txt")
    unit_img, len_img = normalize(images)
    img_bf = unit_img.astype(jnp.bfloat16)
    unit_txt, len_txt = normalize(texts)
    txt_bf = lax.all_gather(unit_txt.astype(jnp.bfloat16), "img", axis=0, tiled=True)
    txt_block = txt_bf.shape[0]
    total = float(img_block * lax.axis_size("img"))
    scores = logit_scale * lax.dot_general(
        img_bf, txt_bf, (((1,), (1,)), ((), ())), preferred_element_type=jnp.float32
    )
    kernel = jnp.exp(scores - logit_scale)
    row_weight = jnp.ones((img_block,), jnp.float32)
    col_scale = jnp.ones((txt_block,), jnp.float32)
    col_total = col_scale
    row_total = row_weight
    last_cols = col_scale
    for step in range(ROUNDS + 1):
        col_part = jnp.dot(row_weight, kernel, precision=highest)
        col_sum = lax.psum(col_part, "img")
        if step == 0:
            col_total = col_sum
        if step == ROUNDS:
            last_cols = col_sum
        else:
            col_scale = 1.0 / (total * col_sum)
            row_part = jnp.dot(kernel, col_scale, precision=highest)
            if step == 0:
                stats = jnp.stack([row_part, jnp.sum(kernel, axis=1)])
            else:
                stats = row_part[None, :]
            summed = lax.psum(stats, "txt")
            if step == 0:
                row_total = summed[1]
            row_weight = 1.0 / (total * summed[0])
    col_weight = 1.0 - mix_weight + mix_weight * total * col_scale * last_cols
    img_ids = img_index * img_block + jnp.arange(img_block, dtype=jnp.int32)
    txt_ids = txt_index * txt_block + jnp.arange(txt_block, dtype=jnp.int32)
    eye = (img_ids[:, None] == txt_ids[None, :]).astype(jnp.float32)
    target = (1.0 - mix_weight) * eye + mix_weight * total * row_weight[
        :, None
    ] * kernel * col_scale[None, :]
    grad_logit = 0.5 * (
        kernel / row_total[:, None]
        + col_weight[None, :] * kernel / col_total[None, :]
        - 2.0 * target
    )
    grad_logit = grad_logit.astype(jnp.bfloat16)
    g_img = lax.psum_scatter(
        logit_scale * jnp.dot(grad_logit, txt_bf, preferred_element_type=jnp.float32),
        "txt",
        scatter_dimension=0,
        tiled=True,
    )
    g_txt = lax.psum_scatter(
        logit_scale
        * lax.dot_general(
            grad_logit, img_bf, (((0,), (0,)), ((), ())), preferred_element_type=jnp.float32
        ),
        "img",
        scatter_dimension=0,
        tiled=True,
    )
    own_unit = lax.dynamic_slice_in_dim(unit_img, txt_index * own_rows, own_rows, 0)
    own_len = lax.dynamic_slice_in_dim(len_img, txt_index * own_rows, own_rows, 0)
    grad_images = project_back(g_img, own_unit, own_len)
    grad_texts = project_back(g_txt, unit_txt, len_txt)
    return (grad_images, grad_texts)


MESH = pl.DeviceIdType.MESH
F32 = jnp.float32
BF16 = jnp.bfloat16
power_scale = logit_scale * 1.4426950408889634


def shifted_exp(scores):
    return jnp.exp2(scores * power_scale - power_scale)


def scaled_kernel(left, right):
    return shifted_exp(jnp.dot(left, right, preferred_element_type=F32))


def fold_rows(values):
    rows, cols = values.shape
    return jnp.sum(values.reshape(rows // 8, 8, cols), axis=0)


def gathered_body(
    images_ref,
    texts_ref,
    grad_ref,
    img_buf,
    txt_buf,
    col_in,
    wide_img,
    raw_img,
    raw_txt,
    kt,
    first_scale,
    img_turned,
    own_turned,
    own_scores,
    send_sem,
    img_recv,
    txt_recv,
    col_recv,
    load_sem,
):
    slots, slot_rows, width = img_buf.shape
    depth, own = col_in.shape[0], texts_ref.shape[0]
    half = width // 2
    total_rows = slots * slot_rows
    chunks = img_recv.shape[1]
    piece = slot_rows // chunks

    load_txt = pltpu.make_async_copy(texts_ref, raw_txt, load_sem.at[0])
    load_txt.start()
    load_img = pltpu.make_async_copy(images_ref, raw_img, load_sem.at[1])
    load_img.start()

    me = lax.axis_index("img")
    layer = lax.axis_index("txt")
    core = me % 2
    x = (me // 2) % 2
    y = me // 4
    first = (y + core * (1 - 2 * y)) * 4 + (x + (1 - core) * (1 - 2 * x)) * 2 + core
    second = (y + (1 - core) * (1 - 2 * y)) * 4 + (x + core * (1 - 2 * x)) * 2 + core
    across = (1 - y) * 4 + (1 - x) * 2 + core
    flip = 1 - 2 * core
    sibling = me + flip

    barrier = pltpu.get_barrier_semaphore()
    for peer in (first, second, sibling):
        pl.semaphore_signal(barrier, inc=1, device_id=(peer, layer), device_id_type=MESH)
    for step in range(1, depth):
        pl.semaphore_signal(
            barrier, inc=1, device_id=(me, (layer + step) % depth), device_id_type=MESH
        )

    load_txt.wait()
    unit_txt, len_txt = normalize(raw_txt[...])
    col_in[layer] = jnp.concatenate([unit_txt[:, :half], unit_txt[:, half:]], axis=0).astype(
        BF16
    )
    pl.semaphore_wait(barrier, 2 + depth)

    started = []

    def push(src, dst, recv, device):
        copy = pltpu.make_async_remote_copy(
            src_ref=src,
            dst_ref=dst,
            send_sem=send_sem.at[len(started)],
            recv_sem=recv,
            device_id=device,
            device_id_type=MESH,
        )
        copy.start()
        started.append(copy)

    settled = []

    def settle(index):
        index = index % len(started)
        for copy in started[index : index + 2 * chunks : 2]:
            copy.wait_send()
            settled.append(copy)

    def part(buf, slot, chunk):
        return buf.at[slot, pl.ds(chunk * piece, piece)]

    def send(buf, slot, chunk, recv, *peers):
        for peer in peers:
            ref = part(buf, slot, chunk)
            push(ref, ref, recv.at[slot, chunk], (peer, layer))

    def landed(ref, recv):
        pltpu.make_async_remote_copy(
            src_ref=ref,
            dst_ref=ref,
            send_sem=send_sem.at[0],
            recv_sem=recv,
            device_id=(sibling, layer),
            device_id_type=MESH,
        ).wait_recv()

    def arrive(buf, slot, recv, *peers):
        for chunk in range(chunks):
            landed(part(buf, slot, chunk), recv.at[slot, chunk])
            send(buf, slot, chunk, recv, *peers)

    for step in range(1, depth):
        push(
            col_in.at[layer],
            col_in.at[layer],
            col_recv.at[layer],
            (me, (layer + step) % depth),
        )
    load_img.wait()
    for chunk in range(chunks):
        rows = pl.ds(chunk * piece, piece)
        wide = raw_img[rows, :].astype(F32)
        wide_img[rows, :] = wide
        unit_part, _ = normalize(wide)
        img_buf[me, rows] = unit_part.astype(BF16)
        send(img_buf, me, chunk, img_recv, first, sibling)
    settle(-2 * chunks)
    for chunk in range(chunks):
        send(img_buf, me, chunk, img_recv, second)

    arrive(img_buf, first, img_recv, second, sibling)
    for step in range(1, depth):
        source = (layer + step) % depth
        landed(col_in.at[source], col_recv.at[source])
    pieces = []
    for z in range(depth):
        block = col_in[z].astype(F32)
        pieces.append(jnp.concatenate([block[:own], block[own:]], axis=1))
    txt_buf[me] = jnp.concatenate(pieces, axis=0).astype(BF16)
    for chunk in range(chunks):
        send(txt_buf, me, chunk, txt_recv, first, sibling)
    text_start = len(started) - 2 * chunks

    arrive(img_buf, second, img_recv, sibling)
    arrive(img_buf, across, img_recv, sibling)
    settle(text_start)
    for chunk in range(chunks):
        send(txt_buf, me, chunk, txt_recv, second)
    arrive(txt_buf, first, txt_recv, second, sibling)
    for slot in (sibling, second + flip, first + flip, across + flip):
        arrive(img_buf, slot, img_recv)

    img_all = img_buf[...].reshape(total_rows, width)
    own_raw = wide_img[pl.ds(pl.multiple_of(layer * own, 8), own), :]
    own_img, len_img = normalize(own_raw)
    img_turned[...] = img_all.T
    padded = jnp.concatenate([own_img, jnp.zeros((128 - own, width), F32)], axis=0)
    own_turned[...] = padded.T.astype(BF16)

    row_acc = jnp.zeros((8, total_rows), F32)
    row_sum = jnp.zeros((8, total_rows), F32)

    def absorb(start, count, row_acc, row_sum):
        block = txt_buf[pl.ds(start, count)].reshape(count * slot_rows, width)
        values = scaled_kernel(block, img_turned[...])
        own_scores[pl.ds(start, count)] = jnp.dot(
            block, own_turned[...], preferred_element_type=F32
        ).reshape(count, slot_rows, 128)
        kt[pl.ds(start, count)] = values.reshape(count, slot_rows, total_rows)
        scale = 1.0 / jnp.sum(values, axis=1, keepdims=True)
        first_scale[pl.ds(start, count)] = scale.reshape(count, slot_rows, 1)
        return row_acc + fold_rows(values * scale), row_sum + fold_rows(values)

    arrive(txt_buf, sibling, txt_recv)
    row_acc, row_sum = absorb(me - core, 2, row_acc, row_sum)
    arrive(txt_buf, second, txt_recv, sibling)
    arrive(txt_buf, first + flip, txt_recv)
    row_acc, row_sum = absorb(first - core, 2, row_acc, row_sum)
    arrive(txt_buf, across, txt_recv, sibling)
    arrive(txt_buf, second + flip, txt_recv)
    row_acc, row_sum = absorb(second - core, 2, row_acc, row_sum)
    row_acc, row_sum = absorb(across, 1, row_acc, row_sum)
    arrive(txt_buf, across + flip, txt_recv)
    row_acc, row_sum = absorb(across + flip, 1, row_acc, row_sum)

    row_total = jnp.sum(row_sum, axis=0, keepdims=True)
    row_weight = 1.0 / jnp.sum(row_acc, axis=0, keepdims=True)
    previous = row_weight
    scales = []
    for step in range(1, ROUNDS):
        previous = row_weight
        row_acc = jnp.zeros((8, total_rows), F32)
        scales = []
        for slot in range(slots):
            scale = 1.0 / jnp.sum(kt[slot] * row_weight, axis=1, keepdims=True)
            row_acc += fold_rows(kt[slot] * scale)
            scales.append(scale)
        row_weight = 1.0 / jnp.sum(row_acc, axis=0, keepdims=True)

    keep = 1.0 - mix_weight
    lane = lax.broadcasted_iota(jnp.int32, (slot_rows, 128), 1)
    packed = []
    for slot in range(slots):
        last_cols = jnp.sum(kt[slot] * row_weight, axis=1, keepdims=True)
        weight = (keep + mix_weight * scales[slot] * last_cols) * first_scale[slot]
        packed.append(jnp.where(lane < 64, scales[slot], weight))
    packed = jnp.concatenate(packed, axis=0).T
    col_scale = packed[0:1]
    col_part = packed[64:65]

    at_row = lax.broadcasted_iota(jnp.int32, (own, total_rows), 0)
    at_col = lax.broadcasted_iota(jnp.int32, (own, total_rows), 1)

    def logit_grad(values, factor, place):
        eye = (at_col == at_row + place).astype(F32)
        return (0.5 * (values * factor - (2.0 * keep) * eye)).astype(BF16)

    values = scaled_kernel(unit_txt.astype(BF16), img_turned[...])
    own_total = jnp.sum(values, axis=1, keepdims=True)
    own_scale = 1.0 / jnp.sum(values * previous, axis=1, keepdims=True)
    own_cols = jnp.sum(values * row_weight, axis=1, keepdims=True)
    own_part = (keep + mix_weight * own_scale * own_cols) / own_total
    factor = 1.0 / row_total + own_part - (2.0 * mix_weight) * (row_weight * own_scale)
    grad_logit = logit_grad(values, factor, layer * (slots * own) + me * own)
    g_txt = logit_scale * jnp.dot(grad_logit, img_all, preferred_element_type=F32)
    grad_ref[own:] = project_back(g_txt, unit_txt, len_txt)

    txt_all = txt_buf[...].reshape(total_rows, width)
    scores = own_scores[...].reshape(total_rows, 128).T[:own]
    values = shifted_exp(scores)
    own_total = jnp.sum(values, axis=1, keepdims=True)
    own_weight = 1.0 / jnp.sum(values * col_scale, axis=1, keepdims=True)
    group = me * depth + layer
    place = (group % slots) * slot_rows + (group // slots) * own
    factor = 1.0 / own_total + col_part - (2.0 * mix_weight) * (own_weight * col_scale)
    grad_logit = logit_grad(values, factor, place)
    g_img = logit_scale * jnp.dot(grad_logit, txt_all, preferred_element_type=F32)
    grad_ref[:own] = project_back(g_img, own_img, len_img)

    for copy in started:
        if not any(copy is other for other in settled):
            copy.wait_send()


def gathered(slots, depth, images, texts):
    slot_rows, width = images.shape
    own = texts.shape[0]
    total_rows = slots * slot_rows
    chunks = 1
    vmem = pl.BlockSpec(memory_space=pltpu.VMEM)
    anywhere = pl.BlockSpec(memory_space=pltpu.HBM)
    out = jax.ShapeDtypeStruct((2 * own, width), F32)
    packed = pl.pallas_call(
        gathered_body,
        out_shape=out,
        in_specs=[anywhere, anywhere],
        out_specs=vmem,
        scratch_shapes=[
            pltpu.VMEM((slots, slot_rows, width), BF16),
            pltpu.VMEM((slots, slot_rows, width), BF16),
            pltpu.VMEM((depth, 2 * own, width // 2), BF16),
            pltpu.VMEM((slot_rows, width), F32),
            pltpu.VMEM((slot_rows, width), BF16),
            pltpu.VMEM((own, width), BF16),
            pltpu.VMEM((slots, slot_rows, total_rows), F32),
            pltpu.VMEM((slots, slot_rows, 1), F32),
            pltpu.VMEM((width, total_rows), BF16),
            pltpu.VMEM((width, 128), BF16),
            pltpu.VMEM((slots, slot_rows, 128), F32),
            pltpu.SemaphoreType.DMA((depth - 1 + 14 * chunks,)),
            pltpu.SemaphoreType.DMA((slots, chunks)),
            pltpu.SemaphoreType.DMA((slots, chunks)),
            pltpu.SemaphoreType.DMA((depth,)),
            pltpu.SemaphoreType.DMA((2,)),
        ],
        compiler_params=pltpu.CompilerParams(
            collective_id=0, has_side_effects=True, vmem_limit_bytes=32 * 1024 * 1024
        ),
    )(*(pltpu.with_memory_space_constraint(array, pltpu.HBM) for array in (images, texts)))
    return packed[:own], packed[own:]


def solution(mesh):
    placed = (P("img", None), P(("txt", "img"), None))
    slots, depth = mesh.shape["img"], mesh.shape["txt"]

    def body(images, texts):
        pairs = images.shape[0] * slots
        whole = slots == 8 and images.shape[0] % 32 == 0 and texts.shape[0] % 8 == 0
        if whole and pairs * pairs * 4 <= 4 * 1024 * 1024:
            return gathered(slots, depth, images, texts)
        return shards(images, texts)

    return jax.shard_map(
        body,
        mesh=mesh,
        in_specs=placed,
        out_specs=(P(("img", "txt"), None), P(("txt", "img"), None)),
        check_vma=False,
    )
```

```python
import jax
import jax.numpy as jnp
from jax import lax
from jax.experimental import pallas as pl
from jax.experimental.pallas import tpu as pltpu
from jax.sharding import PartitionSpec as P

ROUNDS = 3


logit_scale = 30.0
mix_weight = 0.5
norm_eps = 1e-06
highest = lax.Precision.HIGHEST


def normalize(values):
    wide = values.astype(jnp.float32)
    length = jnp.sqrt(jnp.sum(wide * wide, axis=1, keepdims=True) + norm_eps)
    return (wide / length, length)


def project_back(grad, unit, length):
    along = jnp.sum(unit * grad, axis=1, keepdims=True)
    return (grad - unit * along) / length


def shards(images, texts):
    own_rows = texts.shape[0]
    img_block = images.shape[0]
    img_index = lax.axis_index("img")
    txt_index = lax.axis_index("txt")
    unit_img, len_img = normalize(images)
    img_bf = unit_img.astype(jnp.bfloat16)
    unit_txt, len_txt = normalize(texts)
    txt_bf = lax.all_gather(unit_txt.astype(jnp.bfloat16), "img", axis=0, tiled=True)
    txt_block = txt_bf.shape[0]
    total = float(img_block * lax.axis_size("img"))
    scores = logit_scale * lax.dot_general(
        img_bf, txt_bf, (((1,), (1,)), ((), ())), preferred_element_type=jnp.float32
    )
    kernel = jnp.exp(scores - logit_scale)
    row_weight = jnp.ones((img_block,), jnp.float32)
    col_scale = jnp.ones((txt_block,), jnp.float32)
    col_total = col_scale
    row_total = row_weight
    last_cols = col_scale
    for step in range(ROUNDS + 1):
        col_part = jnp.dot(row_weight, kernel, precision=highest)
        col_sum = lax.psum(col_part, "img")
        if step == 0:
            col_total = col_sum
        if step == ROUNDS:
            last_cols = col_sum
        else:
            col_scale = 1.0 / (total * col_sum)
            row_part = jnp.dot(kernel, col_scale, precision=highest)
            if step == 0:
                stats = jnp.stack([row_part, jnp.sum(kernel, axis=1)])
            else:
                stats = row_part[None, :]
            summed = lax.psum(stats, "txt")
            if step == 0:
                row_total = summed[1]
            row_weight = 1.0 / (total * summed[0])
    col_weight = 1.0 - mix_weight + mix_weight * total * col_scale * last_cols
    img_ids = img_index * img_block + jnp.arange(img_block, dtype=jnp.int32)
    txt_ids = txt_index * txt_block + jnp.arange(txt_block, dtype=jnp.int32)
    eye = (img_ids[:, None] == txt_ids[None, :]).astype(jnp.float32)
    target = (1.0 - mix_weight) * eye + mix_weight * total * row_weight[
        :, None
    ] * kernel * col_scale[None, :]
    grad_logit = 0.5 * (
        kernel / row_total[:, None]
        + col_weight[None, :] * kernel / col_total[None, :]
        - 2.0 * target
    )
    grad_logit = grad_logit.astype(jnp.bfloat16)
    g_img = lax.psum_scatter(
        logit_scale * jnp.dot(grad_logit, txt_bf, preferred_element_type=jnp.float32),
        "txt",
        scatter_dimension=0,
        tiled=True,
    )
    g_txt = lax.psum_scatter(
        logit_scale
        * lax.dot_general(
            grad_logit, img_bf, (((0,), (0,)), ((), ())), preferred_element_type=jnp.float32
        ),
        "img",
        scatter_dimension=0,
        tiled=True,
    )
    own_unit = lax.dynamic_slice_in_dim(unit_img, txt_index * own_rows, own_rows, 0)
    own_len = lax.dynamic_slice_in_dim(len_img, txt_index * own_rows, own_rows, 0)
    grad_images = project_back(g_img, own_unit, own_len)
    grad_texts = project_back(g_txt, unit_txt, len_txt)
    return (grad_images, grad_texts)


MESH = pl.DeviceIdType.MESH
F32 = jnp.float32
BF16 = jnp.bfloat16
power_scale = logit_scale * 1.4426950408889634


def shifted_exp(scores):
    return jnp.exp2(scores * power_scale - power_scale)


def scaled_kernel(left, right):
    return shifted_exp(jnp.dot(left, right, preferred_element_type=F32))


def fold_rows(values):
    rows, cols = values.shape
    return jnp.sum(values.reshape(rows // 8, 8, cols), axis=0)


def gathered_body(
    images_ref,
    texts_ref,
    grad_ref,
    img_buf,
    txt_buf,
    col_in,
    wide_img,
    raw_img,
    raw_txt,
    kt,
    first_scale,
    img_turned,
    own_turned,
    own_scores,
    send_sem,
    img_recv,
    txt_recv,
    col_recv,
    load_sem,
):
    slots, slot_rows, width = img_buf.shape
    depth, own = col_in.shape[0], texts_ref.shape[0]
    half = width // 2
    total_rows = slots * slot_rows
    chunks = img_recv.shape[1]
    piece = slot_rows // chunks

    load_txt = pltpu.make_async_copy(texts_ref, raw_txt, load_sem.at[0])
    load_txt.start()
    load_img = pltpu.make_async_copy(images_ref, raw_img, load_sem.at[1])
    load_img.start()

    me = lax.axis_index("img")
    layer = lax.axis_index("txt")
    core = me % 2
    x = (me // 2) % 2
    y = me // 4
    first = (y + core * (1 - 2 * y)) * 4 + (x + (1 - core) * (1 - 2 * x)) * 2 + core
    second = (y + (1 - core) * (1 - 2 * y)) * 4 + (x + core * (1 - 2 * x)) * 2 + core
    across = (1 - y) * 4 + (1 - x) * 2 + core
    flip = 1 - 2 * core
    sibling = me + flip

    barrier = pltpu.get_barrier_semaphore()
    for peer in (first, second, sibling):
        pl.semaphore_signal(barrier, inc=1, device_id=(peer, layer), device_id_type=MESH)
    for step in range(1, depth):
        pl.semaphore_signal(
            barrier, inc=1, device_id=(me, (layer + step) % depth), device_id_type=MESH
        )

    load_txt.wait()
    unit_txt, len_txt = normalize(raw_txt[...])
    col_in[layer] = jnp.concatenate([unit_txt[:, :half], unit_txt[:, half:]], axis=0).astype(
        BF16
    )
    pl.semaphore_wait(barrier, 2 + depth)

    started = []

    def push(src, dst, recv, device):
        copy = pltpu.make_async_remote_copy(
            src_ref=src,
            dst_ref=dst,
            send_sem=send_sem.at[len(started)],
            recv_sem=recv,
            device_id=device,
            device_id_type=MESH,
        )
        copy.start()
        started.append(copy)

    def part(buf, slot, chunk):
        return buf.at[slot, pl.ds(chunk * piece, piece)]

    def send(buf, slot, chunk, recv, *peers):
        for peer in peers:
            ref = part(buf, slot, chunk)
            push(ref, ref, recv.at[slot, chunk], (peer, layer))

    def landed(ref, recv):
        pltpu.make_async_remote_copy(
            src_ref=ref,
            dst_ref=ref,
            send_sem=send_sem.at[0],
            recv_sem=recv,
            device_id=(sibling, layer),
            device_id_type=MESH,
        ).wait_recv()

    def arrive(buf, slot, recv, *peers):
        for chunk in range(chunks):
            landed(part(buf, slot, chunk), recv.at[slot, chunk])
            send(buf, slot, chunk, recv, *peers)

    for step in range(1, depth):
        push(
            col_in.at[layer],
            col_in.at[layer],
            col_recv.at[layer],
            (me, (layer + step) % depth),
        )
    load_img.wait()
    for chunk in range(chunks):
        rows = pl.ds(chunk * piece, piece)
        wide = raw_img[rows, :].astype(F32)
        wide_img[rows, :] = wide
        unit_part, _ = normalize(wide)
        img_buf[me, rows] = unit_part.astype(BF16)
        send(img_buf, me, chunk, img_recv, first, second, sibling)

    own_raw = wide_img[pl.ds(pl.multiple_of(layer * own, 8), own), :]
    own_img, len_img = normalize(own_raw)
    padded = jnp.concatenate([own_img, jnp.zeros((128 - own, width), F32)], axis=0)
    own_turned[...] = padded.T.astype(BF16)

    arrive(img_buf, first, img_recv, second, sibling)
    arrive(img_buf, second, img_recv, sibling)
    for step in range(1, depth):
        source = (layer + step) % depth
        landed(col_in.at[source], col_recv.at[source])
    pieces = []
    for z in range(depth):
        block = col_in[z].astype(F32)
        pieces.append(jnp.concatenate([block[:own], block[own:]], axis=1))
    txt_buf[me] = jnp.concatenate(pieces, axis=0).astype(BF16)
    for chunk in range(chunks):
        send(txt_buf, me, chunk, txt_recv, first, second)
    for chunk in range(chunks):
        send(txt_buf, me, chunk, txt_recv, sibling)

    arrive(img_buf, across, img_recv, sibling)
    arrive(txt_buf, first, txt_recv, second, sibling)
    for slot in (sibling, second + flip, first + flip, across + flip):
        arrive(img_buf, slot, img_recv)

    img_all = img_buf[...].reshape(total_rows, width)
    img_turned[...] = img_all.T

    row_acc = jnp.zeros((8, total_rows), F32)
    row_sum = jnp.zeros((8, total_rows), F32)

    def absorb(start, count, row_acc, row_sum):
        block = txt_buf[pl.ds(start, count)].reshape(count * slot_rows, width)
        values = scaled_kernel(block, img_turned[...])
        own_scores[pl.ds(start, count)] = jnp.dot(
            block, own_turned[...], preferred_element_type=F32
        ).reshape(count, slot_rows, 128)
        kt[pl.ds(start, count)] = values.reshape(count, slot_rows, total_rows)
        scale = 1.0 / jnp.sum(values, axis=1, keepdims=True)
        first_scale[pl.ds(start, count)] = scale.reshape(count, slot_rows, 1)
        return row_acc + fold_rows(values * scale), row_sum + fold_rows(values)

    arrive(txt_buf, sibling, txt_recv)
    row_acc, row_sum = absorb(me - core, 2, row_acc, row_sum)
    arrive(txt_buf, second, txt_recv, sibling)
    arrive(txt_buf, first + flip, txt_recv)
    row_acc, row_sum = absorb(first - core, 2, row_acc, row_sum)
    arrive(txt_buf, across, txt_recv, sibling)
    arrive(txt_buf, second + flip, txt_recv)
    row_acc, row_sum = absorb(second - core, 2, row_acc, row_sum)
    row_acc, row_sum = absorb(across, 1, row_acc, row_sum)
    arrive(txt_buf, across + flip, txt_recv)
    row_acc, row_sum = absorb(across + flip, 1, row_acc, row_sum)

    row_total = jnp.sum(row_sum, axis=0, keepdims=True)
    row_weight = 1.0 / jnp.sum(row_acc, axis=0, keepdims=True)
    previous = row_weight
    scales = []
    for step in range(1, ROUNDS):
        previous = row_weight
        row_acc = jnp.zeros((8, total_rows), F32)
        scales = []
        for slot in range(slots):
            scale = 1.0 / jnp.sum(kt[slot] * row_weight, axis=1, keepdims=True)
            row_acc += fold_rows(kt[slot] * scale)
            scales.append(scale)
        row_weight = 1.0 / jnp.sum(row_acc, axis=0, keepdims=True)

    keep = 1.0 - mix_weight
    lane = lax.broadcasted_iota(jnp.int32, (slot_rows, 128), 1)
    packed = []
    for slot in range(slots):
        last_cols = jnp.sum(kt[slot] * row_weight, axis=1, keepdims=True)
        weight = (keep + mix_weight * scales[slot] * last_cols) * first_scale[slot]
        packed.append(jnp.where(lane < 64, scales[slot], weight))
    packed = jnp.concatenate(packed, axis=0).T
    col_scale = packed[0:1]
    col_part = packed[64:65]

    at_row = lax.broadcasted_iota(jnp.int32, (own, total_rows), 0)
    at_col = lax.broadcasted_iota(jnp.int32, (own, total_rows), 1)

    def logit_grad(values, factor, place):
        eye = (at_col == at_row + place).astype(F32)
        return (0.5 * (values * factor - (2.0 * keep) * eye)).astype(BF16)

    values = scaled_kernel(unit_txt.astype(BF16), img_turned[...])
    own_total = jnp.sum(values, axis=1, keepdims=True)
    own_scale = 1.0 / jnp.sum(values * previous, axis=1, keepdims=True)
    own_cols = jnp.sum(values * row_weight, axis=1, keepdims=True)
    own_part = (keep + mix_weight * own_scale * own_cols) / own_total
    factor = 1.0 / row_total + own_part - (2.0 * mix_weight) * (row_weight * own_scale)
    grad_logit = logit_grad(values, factor, layer * (slots * own) + me * own)
    g_txt = logit_scale * jnp.dot(grad_logit, img_all, preferred_element_type=F32)
    grad_ref[own:] = project_back(g_txt, unit_txt, len_txt)

    txt_all = txt_buf[...].reshape(total_rows, width)
    scores = own_scores[...].reshape(total_rows, 128).T[:own]
    values = shifted_exp(scores)
    own_total = jnp.sum(values, axis=1, keepdims=True)
    own_weight = 1.0 / jnp.sum(values * col_scale, axis=1, keepdims=True)
    group = me * depth + layer
    place = (group % slots) * slot_rows + (group // slots) * own
    factor = 1.0 / own_total + col_part - (2.0 * mix_weight) * (own_weight * col_scale)
    grad_logit = logit_grad(values, factor, place)
    g_img = logit_scale * jnp.dot(grad_logit, txt_all, preferred_element_type=F32)
    grad_ref[:own] = project_back(g_img, own_img, len_img)

    for copy in started:
        copy.wait_send()


def gathered(slots, depth, images, texts):
    slot_rows, width = images.shape
    own = texts.shape[0]
    total_rows = slots * slot_rows
    chunks = 1
    vmem = pl.BlockSpec(memory_space=pltpu.VMEM)
    anywhere = pl.BlockSpec(memory_space=pltpu.HBM)
    out = jax.ShapeDtypeStruct((2 * own, width), F32)
    packed = pl.pallas_call(
        gathered_body,
        out_shape=out,
        in_specs=[anywhere, anywhere],
        out_specs=vmem,
        scratch_shapes=[
            pltpu.VMEM((slots, slot_rows, width), BF16),
            pltpu.VMEM((slots, slot_rows, width), BF16),
            pltpu.VMEM((depth, 2 * own, width // 2), BF16),
            pltpu.VMEM((slot_rows, width), F32),
            pltpu.VMEM((slot_rows, width), BF16),
            pltpu.VMEM((own, width), BF16),
            pltpu.VMEM((slots, slot_rows, total_rows), F32),
            pltpu.VMEM((slots, slot_rows, 1), F32),
            pltpu.VMEM((width, total_rows), BF16),
            pltpu.VMEM((width, 128), BF16),
            pltpu.VMEM((slots, slot_rows, 128), F32),
            pltpu.SemaphoreType.DMA((depth - 1 + 14 * chunks,)),
            pltpu.SemaphoreType.DMA((slots, chunks)),
            pltpu.SemaphoreType.DMA((slots, chunks)),
            pltpu.SemaphoreType.DMA((depth,)),
            pltpu.SemaphoreType.DMA((2,)),
        ],
        compiler_params=pltpu.CompilerParams(
            collective_id=0, has_side_effects=True, vmem_limit_bytes=32 * 1024 * 1024
        ),
    )(*(pltpu.with_memory_space_constraint(array, pltpu.HBM) for array in (images, texts)))
    return packed[:own], packed[own:]


def solution(mesh):
    placed = (P("img", None), P(("txt", "img"), None))
    slots, depth = mesh.shape["img"], mesh.shape["txt"]

    def body(images, texts):
        pairs = images.shape[0] * slots
        whole = slots == 8 and images.shape[0] % 32 == 0 and texts.shape[0] % 8 == 0
        if whole and pairs * pairs * 4 <= 4 * 1024 * 1024:
            return gathered(slots, depth, images, texts)
        return shards(images, texts)

    return jax.shard_map(
        body,
        mesh=mesh,
        in_specs=placed,
        out_specs=(P(("img", "txt"), None), P(("txt", "img"), None)),
        check_vma=False,
    )
```

```python
import jax
import jax.numpy as jnp
from jax import lax
from jax.experimental import pallas as pl
from jax.experimental.pallas import tpu as pltpu
from jax.sharding import PartitionSpec as P

ROUNDS = 3


logit_scale = 30.0
mix_weight = 0.5
norm_eps = 1e-06
highest = lax.Precision.HIGHEST


def normalize(values):
    wide = values.astype(jnp.float32)
    length = jnp.sqrt(jnp.sum(wide * wide, axis=1, keepdims=True) + norm_eps)
    return (wide / length, length)


def project_back(grad, unit, length):
    along = jnp.sum(unit * grad, axis=1, keepdims=True)
    return (grad - unit * along) / length


def shards(images, texts):
    own_rows = texts.shape[0]
    img_block = images.shape[0]
    img_index = lax.axis_index("img")
    txt_index = lax.axis_index("txt")
    unit_img, len_img = normalize(images)
    img_bf = unit_img.astype(jnp.bfloat16)
    unit_txt, len_txt = normalize(texts)
    txt_bf = lax.all_gather(unit_txt.astype(jnp.bfloat16), "img", axis=0, tiled=True)
    txt_block = txt_bf.shape[0]
    total = float(img_block * lax.axis_size("img"))
    scores = logit_scale * lax.dot_general(
        img_bf, txt_bf, (((1,), (1,)), ((), ())), preferred_element_type=jnp.float32
    )
    kernel = jnp.exp(scores - logit_scale)
    row_weight = jnp.ones((img_block,), jnp.float32)
    col_scale = jnp.ones((txt_block,), jnp.float32)
    col_total = col_scale
    row_total = row_weight
    last_cols = col_scale
    for step in range(ROUNDS + 1):
        col_part = jnp.dot(row_weight, kernel, precision=highest)
        col_sum = lax.psum(col_part, "img")
        if step == 0:
            col_total = col_sum
        if step == ROUNDS:
            last_cols = col_sum
        else:
            col_scale = 1.0 / (total * col_sum)
            row_part = jnp.dot(kernel, col_scale, precision=highest)
            if step == 0:
                stats = jnp.stack([row_part, jnp.sum(kernel, axis=1)])
            else:
                stats = row_part[None, :]
            summed = lax.psum(stats, "txt")
            if step == 0:
                row_total = summed[1]
            row_weight = 1.0 / (total * summed[0])
    col_weight = 1.0 - mix_weight + mix_weight * total * col_scale * last_cols
    img_ids = img_index * img_block + jnp.arange(img_block, dtype=jnp.int32)
    txt_ids = txt_index * txt_block + jnp.arange(txt_block, dtype=jnp.int32)
    eye = (img_ids[:, None] == txt_ids[None, :]).astype(jnp.float32)
    target = (1.0 - mix_weight) * eye + mix_weight * total * row_weight[
        :, None
    ] * kernel * col_scale[None, :]
    grad_logit = 0.5 * (
        kernel / row_total[:, None]
        + col_weight[None, :] * kernel / col_total[None, :]
        - 2.0 * target
    )
    grad_logit = grad_logit.astype(jnp.bfloat16)
    g_img = lax.psum_scatter(
        logit_scale * jnp.dot(grad_logit, txt_bf, preferred_element_type=jnp.float32),
        "txt",
        scatter_dimension=0,
        tiled=True,
    )
    g_txt = lax.psum_scatter(
        logit_scale
        * lax.dot_general(
            grad_logit, img_bf, (((0,), (0,)), ((), ())), preferred_element_type=jnp.float32
        ),
        "img",
        scatter_dimension=0,
        tiled=True,
    )
    own_unit = lax.dynamic_slice_in_dim(unit_img, txt_index * own_rows, own_rows, 0)
    own_len = lax.dynamic_slice_in_dim(len_img, txt_index * own_rows, own_rows, 0)
    grad_images = project_back(g_img, own_unit, own_len)
    grad_texts = project_back(g_txt, unit_txt, len_txt)
    return (grad_images, grad_texts)


MESH = pl.DeviceIdType.MESH
F32 = jnp.float32
BF16 = jnp.bfloat16
power_scale = logit_scale * 1.4426950408889634


def shifted_exp(scores):
    return jnp.exp2(scores * power_scale - power_scale)


def scaled_kernel(left, right):
    return shifted_exp(jnp.dot(left, right, preferred_element_type=F32))


def fold_rows(values):
    rows, cols = values.shape
    return jnp.sum(values.reshape(rows // 8, 8, cols), axis=0)


def gathered_body(
    images_ref,
    texts_ref,
    grad_ref,
    img_buf,
    txt_buf,
    col_in,
    wide_img,
    raw_img,
    raw_txt,
    kt,
    first_scale,
    img_turned,
    own_turned,
    own_scores,
    send_sem,
    img_recv,
    txt_recv,
    col_recv,
    load_sem,
):
    slots, slot_rows, width = img_buf.shape
    depth, own = col_in.shape[0], texts_ref.shape[0]
    half = width // 2
    total_rows = slots * slot_rows
    chunks = img_recv.shape[1]
    piece = slot_rows // chunks

    load_txt = pltpu.make_async_copy(texts_ref, raw_txt, load_sem.at[0])
    load_txt.start()
    load_img = pltpu.make_async_copy(images_ref, raw_img, load_sem.at[1])
    load_img.start()

    me = lax.axis_index("img")
    layer = lax.axis_index("txt")
    core = me % 2
    x = (me // 2) % 2
    y = me // 4
    first = (y + core * (1 - 2 * y)) * 4 + (x + (1 - core) * (1 - 2 * x)) * 2 + core
    second = (y + (1 - core) * (1 - 2 * y)) * 4 + (x + core * (1 - 2 * x)) * 2 + core
    across = (1 - y) * 4 + (1 - x) * 2 + core
    flip = 1 - 2 * core
    sibling = me + flip

    barrier = pltpu.get_barrier_semaphore()
    for peer in (first, second, sibling):
        pl.semaphore_signal(barrier, inc=1, device_id=(peer, layer), device_id_type=MESH)
    for step in range(1, depth):
        pl.semaphore_signal(
            barrier, inc=1, device_id=(me, (layer + step) % depth), device_id_type=MESH
        )

    load_txt.wait()
    unit_txt, len_txt = normalize(raw_txt[...])
    col_in[layer] = jnp.concatenate([unit_txt[:, :half], unit_txt[:, half:]], axis=0).astype(
        BF16
    )
    pl.semaphore_wait(barrier, 2 + depth)

    started = []

    def push(src, dst, recv, device):
        copy = pltpu.make_async_remote_copy(
            src_ref=src,
            dst_ref=dst,
            send_sem=send_sem.at[len(started)],
            recv_sem=recv,
            device_id=device,
            device_id_type=MESH,
        )
        copy.start()
        started.append(copy)

    def part(buf, slot, chunk):
        return buf.at[slot, pl.ds(chunk * piece, piece)]

    def send(buf, slot, chunk, recv, *peers):
        for peer in peers:
            ref = part(buf, slot, chunk)
            push(ref, ref, recv.at[slot, chunk], (peer, layer))

    def landed(ref, recv):
        pltpu.make_async_remote_copy(
            src_ref=ref,
            dst_ref=ref,
            send_sem=send_sem.at[0],
            recv_sem=recv,
            device_id=(sibling, layer),
            device_id_type=MESH,
        ).wait_recv()

    def arrive(buf, slot, recv, *peers):
        for chunk in range(chunks):
            landed(part(buf, slot, chunk), recv.at[slot, chunk])
            send(buf, slot, chunk, recv, *peers)

    for step in range(1, depth):
        push(
            col_in.at[layer],
            col_in.at[layer],
            col_recv.at[layer],
            (me, (layer + step) % depth),
        )
    load_img.wait()
    for chunk in range(chunks):
        rows = pl.ds(chunk * piece, piece)
        wide = raw_img[rows, :].astype(F32)
        wide_img[rows, :] = wide
        unit_part, _ = normalize(wide)
        img_buf[me, rows] = unit_part.astype(BF16)
        send(img_buf, me, chunk, img_recv, first, second, sibling)

    own_raw = wide_img[pl.ds(pl.multiple_of(layer * own, 8), own), :]
    own_img, len_img = normalize(own_raw)
    padded = jnp.concatenate([own_img, jnp.zeros((128 - own, width), F32)], axis=0)
    own_turned[...] = padded.T.astype(BF16)

    arrive(img_buf, first, img_recv, second, sibling)
    arrive(img_buf, second, img_recv, sibling)
    for step in range(1, depth):
        source = (layer + step) % depth
        landed(col_in.at[source], col_recv.at[source])
    pieces = []
    for z in range(depth):
        block = col_in[z].astype(F32)
        pieces.append(jnp.concatenate([block[:own], block[own:]], axis=1))
    txt_buf[me] = jnp.concatenate(pieces, axis=0).astype(BF16)
    for chunk in range(chunks):
        send(txt_buf, me, chunk, txt_recv, first, second)
    for chunk in range(chunks):
        send(txt_buf, me, chunk, txt_recv, sibling)

    arrive(img_buf, across, img_recv, sibling)
    arrive(txt_buf, first, txt_recv, second, sibling)
    for slot in (sibling, second + flip, first + flip, across + flip):
        arrive(img_buf, slot, img_recv)

    img_all = img_buf[...].reshape(total_rows, width)
    img_turned[...] = img_all.T

    row_acc = jnp.zeros((8, total_rows), F32)
    row_sum = jnp.zeros((8, total_rows), F32)

    def absorb(start, count, row_acc, row_sum):
        block = txt_buf[pl.ds(start, count)].reshape(count * slot_rows, width)
        values = scaled_kernel(block, img_turned[...])
        own_scores[pl.ds(start, count)] = jnp.dot(
            block, own_turned[...], preferred_element_type=F32
        ).reshape(count, slot_rows, 128)
        kt[pl.ds(start, count)] = values.reshape(count, slot_rows, total_rows)
        scale = 1.0 / jnp.sum(values, axis=1, keepdims=True)
        first_scale[pl.ds(start, count)] = scale.reshape(count, slot_rows, 1)
        return row_acc + fold_rows(values * scale), row_sum + fold_rows(values)

    arrive(txt_buf, sibling, txt_recv)
    row_acc, row_sum = absorb(me - core, 2, row_acc, row_sum)
    arrive(txt_buf, second, txt_recv, sibling)
    arrive(txt_buf, first + flip, txt_recv)
    row_acc, row_sum = absorb(first - core, 2, row_acc, row_sum)
    arrive(txt_buf, across, txt_recv, sibling)
    arrive(txt_buf, second + flip, txt_recv)
    row_acc, row_sum = absorb(second - core, 2, row_acc, row_sum)
    arrive(txt_buf, across + flip, txt_recv)
    row_acc, row_sum = absorb(across - core, 2, row_acc, row_sum)

    row_total = jnp.sum(row_sum, axis=0, keepdims=True)
    row_weight = 1.0 / jnp.sum(row_acc, axis=0, keepdims=True)
    previous = row_weight
    scales = []
    for step in range(1, ROUNDS):
        previous = row_weight
        row_acc = jnp.zeros((8, total_rows), F32)
        scales = []
        for slot in range(slots):
            scale = 1.0 / jnp.sum(kt[slot] * row_weight, axis=1, keepdims=True)
            row_acc += fold_rows(kt[slot] * scale)
            scales.append(scale)
        row_weight = 1.0 / jnp.sum(row_acc, axis=0, keepdims=True)

    keep = 1.0 - mix_weight
    lane = lax.broadcasted_iota(jnp.int32, (slot_rows, 128), 1)
    packed = []
    for slot in range(slots):
        last_cols = jnp.sum(kt[slot] * row_weight, axis=1, keepdims=True)
        weight = (keep + mix_weight * scales[slot] * last_cols) * first_scale[slot]
        packed.append(jnp.where(lane < 64, scales[slot], weight))
    packed = jnp.concatenate(packed, axis=0).T
    col_scale = packed[0:1]
    col_part = packed[64:65]

    at_row = lax.broadcasted_iota(jnp.int32, (own, total_rows), 0)
    at_col = lax.broadcasted_iota(jnp.int32, (own, total_rows), 1)

    def logit_grad(values, factor, place):
        eye = (at_col == at_row + place).astype(F32)
        return (0.5 * (values * factor - (2.0 * keep) * eye)).astype(BF16)

    values = scaled_kernel(unit_txt.astype(BF16), img_turned[...])
    own_total = jnp.sum(values, axis=1, keepdims=True)
    own_scale = 1.0 / jnp.sum(values * previous, axis=1, keepdims=True)
    own_cols = jnp.sum(values * row_weight, axis=1, keepdims=True)
    own_part = (keep + mix_weight * own_scale * own_cols) / own_total
    factor = 1.0 / row_total + own_part - (2.0 * mix_weight) * (row_weight * own_scale)
    grad_logit = logit_grad(values, factor, layer * (slots * own) + me * own)
    g_txt = logit_scale * jnp.dot(grad_logit, img_all, preferred_element_type=F32)
    grad_ref[own:] = project_back(g_txt, unit_txt, len_txt)

    txt_all = txt_buf[...].reshape(total_rows, width)
    scores = own_scores[...].reshape(total_rows, 128).T[:own]
    values = shifted_exp(scores)
    own_total = jnp.sum(values, axis=1, keepdims=True)
    own_weight = 1.0 / jnp.sum(values * col_scale, axis=1, keepdims=True)
    group = me * depth + layer
    place = (group % slots) * slot_rows + (group // slots) * own
    factor = 1.0 / own_total + col_part - (2.0 * mix_weight) * (own_weight * col_scale)
    grad_logit = logit_grad(values, factor, place)
    g_img = logit_scale * jnp.dot(grad_logit, txt_all, preferred_element_type=F32)
    grad_ref[:own] = project_back(g_img, own_img, len_img)

    for copy in started:
        copy.wait_send()


def gathered(slots, depth, images, texts):
    slot_rows, width = images.shape
    own = texts.shape[0]
    total_rows = slots * slot_rows
    chunks = 1
    vmem = pl.BlockSpec(memory_space=pltpu.VMEM)
    anywhere = pl.BlockSpec(memory_space=pltpu.HBM)
    out = jax.ShapeDtypeStruct((2 * own, width), F32)
    packed = pl.pallas_call(
        gathered_body,
        out_shape=out,
        in_specs=[anywhere, anywhere],
        out_specs=vmem,
        scratch_shapes=[
            pltpu.VMEM((slots, slot_rows, width), BF16),
            pltpu.VMEM((slots, slot_rows, width), BF16),
            pltpu.VMEM((depth, 2 * own, width // 2), BF16),
            pltpu.VMEM((slot_rows, width), F32),
            pltpu.VMEM((slot_rows, width), BF16),
            pltpu.VMEM((own, width), BF16),
            pltpu.VMEM((slots, slot_rows, total_rows), F32),
            pltpu.VMEM((slots, slot_rows, 1), F32),
            pltpu.VMEM((width, total_rows), BF16),
            pltpu.VMEM((width, 128), BF16),
            pltpu.VMEM((slots, slot_rows, 128), F32),
            pltpu.SemaphoreType.DMA((depth - 1 + 14 * chunks,)),
            pltpu.SemaphoreType.DMA((slots, chunks)),
            pltpu.SemaphoreType.DMA((slots, chunks)),
            pltpu.SemaphoreType.DMA((depth,)),
            pltpu.SemaphoreType.DMA((2,)),
        ],
        compiler_params=pltpu.CompilerParams(
            collective_id=0, has_side_effects=True, vmem_limit_bytes=32 * 1024 * 1024
        ),
    )(*(pltpu.with_memory_space_constraint(array, pltpu.HBM) for array in (images, texts)))
    return packed[:own], packed[own:]


def solution(mesh):
    placed = (P("img", None), P(("txt", "img"), None))
    slots, depth = mesh.shape["img"], mesh.shape["txt"]

    def body(images, texts):
        pairs = images.shape[0] * slots
        whole = slots == 8 and images.shape[0] % 32 == 0 and texts.shape[0] % 8 == 0
        if whole and pairs * pairs * 4 <= 4 * 1024 * 1024:
            return gathered(slots, depth, images, texts)
        return shards(images, texts)

    return jax.shard_map(
        body,
        mesh=mesh,
        in_specs=placed,
        out_specs=(P(("img", "txt"), None), P(("txt", "img"), None)),
        check_vma=False,
    )
```
